128 devices in a mesh: ctx: 4 (over z), tp: 32 (over x, y, core).
Axes of the slice: x: 4, y: 4, z: 4, core: 2. Of those that a mesh axis runs over, the one named last changes fastest.
Arguments:
- conv_out: bfloat16 [1024, 16384], P('ctx', 'tp'), may hold values from -6 to 6
- gate_in: bfloat16 [1024, 16384], P('ctx', 'tp'), may hold values from -6 to 6
- residual: bfloat16 [1024, 8192], P('ctx', 'tp')
- xproj_weight: bfloat16 [16384, 544], P('tp'), may hold values from -0.046875 to 0.046875
- dtproj_weight: bfloat16 [512, 16384], P(None, 'tp'), may hold values from -0.25 to 0.25
- dt_bias: float32 [16384], P('tp')
- a_log: float32 [16, 16384], P(None, 'tp'), may hold values from 0 to 2.77
- d_skip: float32 [16384], P('tp'), may hold values from 0.5 to 1.5
- init_state: float32 [16, 16384], P(None, 'tp'), may hold values from -2 to 2
- out_weight: bfloat16 [16384, 8192], P('tp'), may hold values from -0.09375 to 0.09375
- norm_gain: float32 [8192], P('tp'), may hold values from 0.1 to 1.9
- kv_weight: bfloat16 [8192, 2048], P('tp'), may hold values from -0.125 to 0.125
- owner: int32 [128], replicated, may hold values from 0 to 127, each once
- block_start: int32 [128], replicated, may hold values from 0 to 5, as said below
- block_count: int32 [128], replicated, may hold values from 3 to 4, as said below
Outputs:
- layer_out: bfloat16 [1024, 8192], P('ctx', 'tp')
- kv_cache: bfloat16 [128, 4, 16, 128, 128], P(('ctx', 'tp'))
The draws below stay inside these ranges and needn't reach their ends.
Inputs may be any that keep to these rules, and one draw needn't show every extreme that they name: Each request's blocks lie in the window: block_start + block_count <= 8. `block_count`: some request has exactly 4 blocks.
All inputs are finite; a program needn't handle non-finite values.
Results may differ from the reference program's by a relative error of at most 0.033.
Values may be sent and summed in bfloat16 or wider, within the bound.
No kernel may reach another device: no remote copies, remote signals or barrier semaphores. Data moves between devices by JAX's collectives and lax.ppermute only.
A program may use at most 128 MiB of HBM per device.

```python
import math
import jax
import jax.numpy as jnp
from jax import lax

D = 8192
INNER = 16384
STATE = 16
DTR = 512
KVH = 8
HEAD = 128
BLK = 128
TOKENS = 1024
BLOCKS = 8
CAP = 4
N_TP = 32
DEVICES = 128


def request_ranges(key):
    count_key = jax.random.fold_in(key, 21)
    start_key = jax.random.fold_in(key, 22)
    chosen_key = jax.random.fold_in(key, 23)
    least = CAP - CAP // 4
    counts = jax.random.randint(count_key, (DEVICES,), least, CAP + 1)
    chosen = jax.random.randint(chosen_key, (), 0, DEVICES)
    following = (chosen + 1) % DEVICES
    indices = jnp.arange(DEVICES)
    counts = jnp.where(indices == chosen, CAP, counts)
    counts = jnp.where(indices == following, least, counts).astype(jnp.int32)
    starts = jax.random.randint(start_key, (DEVICES,), 0, BLOCKS - counts + 1)
    starts = jnp.where(indices == chosen, 0, starts)
    starts = jnp.where(indices == following, BLOCKS - least, starts).astype(jnp.int32)
    return (starts, counts)


def draw_block_start(key, part):
    shared = request_ranges(key)
    return shared[0]


def draw_block_count(key, part):
    shared = request_ranges(key)
    return shared[1]


def draw_residual(key, part):
    key = jax.random.fold_in(key, 5)
    base_key, row_key = jax.random.split(key)
    row_scale = 10.0 ** (jax.random.uniform(row_key, (TOKENS, 1), jnp.float32) - 0.75)
    base = jax.random.normal(base_key, (TOKENS, D), jnp.float32)
    column_scale = 10.0 ** (jnp.arange(D, dtype=jnp.float32) / D - 0.75)
    return (jnp.clip(base, -4.0, 4.0) * row_scale * column_scale[None, :]).astype(jnp.bfloat16)


def mixed_steps(key, share, slow_low, slow_high, fast_low, fast_high):
    pick_key, slow_key, fast_key = jax.random.split(key, 3)
    slow_part = jax.random.uniform(slow_key, (INNER,), jnp.float32, math.log(slow_low), math.log(slow_high))
    fast_part = jax.random.uniform(fast_key, (INNER,), jnp.float32, math.log(fast_low), math.log(fast_high))
    picked = jax.random.uniform(pick_key, (INNER,), jnp.float32) < share
    return jnp.exp(jnp.where(picked, fast_part, slow_part))


def draw_dt_bias(key, part):
    key = jax.random.fold_in(key, 6)
    base_step = mixed_steps(key, 0.4, 1e-05, 0.003, 0.01, 0.1)
    return jnp.log(jnp.expm1(base_step))


def strengthened(values, own_key, source, target, shards_of, factor):
    def block_of(position):
        return (jnp.arange(values.shape[position]) // (values.shape[position] // shards_of)).reshape((-1,) + (1,) * (values.ndim - 1 - position))

    near = jax.random.permutation(own_key, shards_of)[block_of(target)]
    far = (block_of(target) + shards_of // 2) % shards_of
    return jnp.where((block_of(source) == near) | (block_of(source) == far), factor * values, values)


def block_levels(own_key, dims, shards, smallest, largest):
    def one(axis_at, parts):
        steps = jax.random.uniform(jax.random.fold_in(jax.random.fold_in(own_key, 6), axis_at), (parts,), jnp.float32, smallest / len(shards), largest / len(shards))
        return jnp.repeat(jnp.exp(steps), dims[axis_at] // parts).reshape((-1,) + (1,) * (len(dims) - axis_at - 1))

    level = one(*shards[0])
    for cut in shards[1:]:
        level = level * one(*cut)
    return level


def gaussian(own_key, dims, width, reach, cuts=(), kind=jnp.bfloat16):
    level = block_levels(own_key, dims, cuts, -0.22, 0.18) if cuts else 1.0
    values = jax.random.normal(own_key, dims, jnp.float32) * width * level
    return jnp.minimum(jnp.maximum(values, -reach), reach).astype(kind)


def heavy_noise(stream_key, dims, width, most, shards, heavy, kind=jnp.bfloat16):
    result = width * jax.random.normal(stream_key, dims, jnp.float32)
    if shards:
        result = result * block_levels(stream_key, dims, shards, -0.22, 0.18)
    return jnp.clip(strengthened(result, jax.random.fold_in(stream_key, 3), *heavy), -most, most).astype(kind)


def setup_inputs(seed: int = 0) -> dict:
    seeds = jax.random.split(jax.random.key(seed), 16)
    conv_out = gaussian(seeds[0], (TOKENS, INNER), 1.0, 6.0, ((0, 4), (1, 32)))
    gate_in = gaussian(seeds[1], (TOKENS, INNER), 1.0, 6.0, ((0, 4), (1, 32)))
    residual = draw_residual(jax.random.fold_in(seeds[15], 71), 0)
    xproj_weight = gaussian(seeds[3], (INNER, DTR + 2 * STATE), INNER ** -0.5, 0.046875, ((0, 32),))
    dtproj_weight = gaussian(seeds[4], (DTR, INNER), DTR ** -0.5, 0.25, ((1, 32),))
    dt_bias = draw_dt_bias(jax.random.fold_in(seeds[15], 71), 0)
    a_log = jnp.clip(2.77 * jax.random.uniform(seeds[6], (STATE, INNER), jnp.float32) ** block_levels(seeds[6], (STATE, INNER), ((1, 32),), -0.2, 0.2), 0.0, 2.77)
    d_skip = jnp.clip(0.5 + 1.0 * jax.random.uniform(seeds[7], (INNER,), jnp.float32) ** block_levels(seeds[7], (INNER,), ((0, 32),), -0.2, 0.2), 0.5, 1.5)
    init_state = gaussian(seeds[8], (STATE, INNER), 0.3, 2.0, ((1, 32),), jnp.float32)
    out_weight = heavy_noise(seeds[9], (INNER, D), INNER ** -0.5, 0.09375, ((0, 32),), (0, 1, 32, 2.75))
    norm_gain = jnp.clip(1.0 + 0.18 * jax.random.normal(seeds[10], (D,), jnp.float32), 0.1, 1.9)
    kv_weight = heavy_noise(seeds[11], (D, 2 * KVH * HEAD), D ** -0.5, 0.125, ((0, 32),), (0, 1, 32, 2.75))
    owner = jax.random.permutation(seeds[12], DEVICES).astype(jnp.int32)
    block_start = draw_block_start(jax.random.fold_in(seeds[15], 71), 0)
    block_count = draw_block_count(jax.random.fold_in(seeds[15], 71), 0)
    return {"conv_out": conv_out, "gate_in": gate_in, "residual": residual, "xproj_weight": xproj_weight, "dtproj_weight": dtproj_weight, "dt_bias": dt_bias, "a_log": a_log, "d_skip": d_skip, "init_state": init_state, "out_weight": out_weight, "norm_gain": norm_gain, "kv_weight": kv_weight, "owner": owner, "block_start": block_start, "block_count": block_count}


epsilon = 1e-05

def rounded(value):
    return lax.optimization_barrier(value.astype(jnp.bfloat16)).astype(jnp.float32)

def reference(conv_out, gate_in, residual, xproj_weight, dtproj_weight, dt_bias, a_log, d_skip, init_state, out_weight, norm_gain, kv_weight, owner, block_start, block_count):
    projected = jnp.dot(conv_out, xproj_weight, preferred_element_type=jnp.float32)
    low_rank = projected[:, :DTR].astype(jnp.bfloat16)
    state_in = projected[:, DTR:DTR + STATE]
    state_out = projected[:, DTR + STATE:]
    step_size = jax.nn.softplus(jnp.dot(low_rank, dtproj_weight, preferred_element_type=jnp.float32) + dt_bias)
    decay_rate = -jnp.exp(a_log)
    signal = conv_out.astype(jnp.float32)

    def advance(hidden, inputs):
        step_now, signal_now, in_now, out_now = inputs
        hidden = jnp.exp(step_now[None, :] * decay_rate) * hidden + in_now[:, None] * (step_now * signal_now)[None, :]
        return (hidden, lax.optimization_barrier(jnp.sum(hidden * out_now[:, None], axis=0)))
    scanned = lax.scan(advance, init_state, (step_size, signal, state_in, state_out))[1]
    gated = ((scanned + d_skip * signal) * jax.nn.silu(gate_in.astype(jnp.float32))).astype(jnp.bfloat16)
    group = INNER // N_TP
    mixed = jnp.zeros((TOKENS, D), jnp.float32)
    for member in range(N_TP):
        lower = member * group
        mixed = mixed + rounded(jnp.dot(gated[:, lower:lower + group], out_weight[lower:lower + group], preferred_element_type=jnp.float32))
    layer_out = (residual.astype(jnp.float32) + mixed).astype(jnp.bfloat16)
    stream = layer_out.astype(jnp.float32)
    scaled = (stream * norm_gain).astype(jnp.bfloat16)
    feature_group = D // N_TP
    squares = jnp.zeros((TOKENS,), jnp.float32)
    kv_total = jnp.zeros((TOKENS, 2 * KVH * HEAD), jnp.float32)
    for member in range(N_TP):
        lower = member * feature_group
        piece = stream[:, lower:lower + feature_group]
        squares = squares + rounded(lax.optimization_barrier(jnp.sum(piece * piece, axis=1)))
        kv_total = kv_total + rounded(jnp.dot(scaled[:, lower:lower + feature_group], kv_weight[lower:lower + feature_group], preferred_element_type=jnp.float32))
    keys_values = (kv_total * lax.rsqrt(squares / D + epsilon)[:, None]).astype(jnp.bfloat16)
    tiles = keys_values.reshape(BLOCKS, BLK, 2 * KVH, HEAD).transpose(0, 2, 1, 3)
    padded = jnp.concatenate([tiles, jnp.zeros((CAP, 2 * KVH, BLK, HEAD), jnp.bfloat16)], axis=0)
    owners_all = jnp.arange(DEVICES, dtype=jnp.int32)
    matches = owner[:, None] == owners_all[None, :]
    starts = lax.optimization_barrier(jnp.sum(jnp.where(matches, block_start[:, None], 0), axis=0)).astype(jnp.int32)
    counts = lax.optimization_barrier(jnp.sum(jnp.where(matches, block_count[:, None], 0), axis=0)).astype(jnp.int32)
    slots = jnp.arange(CAP, dtype=jnp.int32)

    def fetch(request):
        window = lax.dynamic_slice_in_dim(padded, request[0].astype(jnp.int32), CAP, 0)
        return jnp.where((slots < request[1])[:, None, None, None], window, jnp.zeros_like(window))
    kv_cache = lax.map(fetch, (starts, counts))
    return (layer_out, kv_cache)
```

```python
import jax
import jax.numpy as jnp
from jax import lax
from jax.experimental import pallas as pl
from jax.experimental.pallas import tpu as pltpu
from jax.sharding import PartitionSpec as P

D = 8192
STATE = 16
DTR = 512
KVH = 8
HEAD = 128
BLK = 128
CAP = 4
EPS = 1e-05
LOG2E = 1.4426950408889634
CHUNK = 32
BF = jnp.bfloat16
F32 = jnp.float32

VM = pl.BlockSpec(memory_space=pltpu.VMEM)
SM = pl.BlockSpec(memory_space=pltpu.SMEM)
ANY = pl.BlockSpec(memory_space=pl.ANY)


def params(mib):
    return pltpu.CompilerParams(vmem_limit_bytes=mib * 1024 * 1024)


def project_kernel(conv_ref, weight_ref, out_ref):
    out_ref[...] = lax.dot_general(
        conv_ref[...], weight_ref[...], (((1,), (1,)), ((), ())), preferred_element_type=F32
    ).astype(BF)


def advance_block(block, hidden, step_ref, drive_ref, states_ref, rates, read_out):
    states = states_ref[block]
    for group in range(CHUNK // 8):
        rows = pl.ds(pl.multiple_of(block * CHUNK + group * 8, 8), 8)
        steps, drives = step_ref[rows, :], drive_ref[rows, :]
        outs = []
        for i in range(8):
            at = group * 8 + i
            decay = jnp.exp2(steps[i : i + 1, :] * rates)
            hidden = decay * hidden + states[:STATE, at : at + 1] * drives[i : i + 1, :]
            if read_out is not None:
                outs.append(
                    jnp.sum(hidden * states[STATE:, at : at + 1], axis=0, keepdims=True)
                )
        if read_out is not None:
            read_out[rows, :] = jnp.concatenate(outs, axis=0)
    return hidden


def first_kernel(
    proj_ref, weight_ref, bias_ref, alog_ref, conv_ref,
    step_ref, states_ref, ends_ref, wide_ref, drive_ref,
):
    tokens = step_ref.shape[0]
    wide_ref[:, : 2 * STATE] = proj_ref[:, DTR:].astype(F32)
    flipped = jnp.transpose(wide_ref[...])
    for block in range(tokens // CHUNK):
        states_ref[block] = flipped[: 2 * STATE, block * CHUNK : (block + 1) * CHUNK]
    step = jax.nn.softplus(
        jnp.dot(proj_ref[:, :DTR], weight_ref[...], preferred_element_type=F32) + bias_ref[...]
    )
    step_ref[...] = step
    drive_ref[...] = step * conv_ref[...].astype(F32)
    rates = -jnp.exp(alog_ref[...]) * LOG2E
    hidden = lax.fori_loop(
        0,
        tokens // CHUNK,
        lambda k, h: advance_block(k, h, step_ref, drive_ref, states_ref, rates, None),
        jnp.zeros_like(rates),
    )
    ends_ref[:STATE, :] = hidden
    ends_ref[STATE:, :] = jnp.broadcast_to(jnp.sum(step, axis=0, keepdims=True), (8, step.shape[1]))


def second_kernel(
    place_ref, step_ref, states_ref, alog_ref, conv_ref, gate_ref, skip_ref, init_ref,
    near_ref, mid_ref, far_ref, weight_ref,
    keep_ref, give_ref, drive_ref, scan_ref, held_ref, sems,
):
    tokens = step_ref.shape[0]
    place, core = place_ref[0], place_ref[1]
    pairs = keep_ref.shape[0]
    wide = held_ref.shape[3]

    def fetch(side, pair):
        which = core if side == 1 else 1 - core
        columns = pl.ds(pl.multiple_of((2 * pair + which) * wide, wide), wide)
        return pltpu.make_async_copy(
            weight_ref.at[:, columns], held_ref.at[side, pair], sems.at[side, pair]
        )

    for side in range(2):
        for pair in range(pairs):
            fetch(side, pair).start()

    rates = -jnp.exp(alog_ref[...]) * LOG2E
    hidden = init_ref[...]
    for back, ref in ((3, far_ref), (2, mid_ref), (1, near_ref)):
        passed = jnp.exp2(ref[STATE : STATE + 1, :] * rates) * hidden + ref[:STATE, :]
        hidden = jnp.where(place >= back, passed, hidden)
    drive_ref[...] = step_ref[...] * conv_ref[...].astype(F32)
    lax.fori_loop(
        0,
        tokens // CHUNK,
        lambda k, h: advance_block(k, h, step_ref, drive_ref, states_ref, rates, scan_ref),
        hidden,
    )
    gate = gate_ref[...].astype(F32)
    gated = (
        (scan_ref[...] + skip_ref[...] * conv_ref[...].astype(F32)) * (gate / (1.0 + jnp.exp(-gate)))
    ).astype(BF)
    for side, ref in ((0, give_ref), (1, keep_ref)):
        for pair in range(pairs):
            fetch(side, pair).wait()
            ref[pair] = jnp.dot(
                gated, held_ref[side, pair], preferred_element_type=F32
            ).astype(BF)


def layer_kernel(parts_ref, residual_ref, gain_ref, weight_ref, layer_ref, out_ref):
    mixed = jnp.sum(parts_ref[...].astype(F32), axis=0)
    layer = (residual_ref[...].astype(F32) + mixed).astype(BF)
    layer_ref[...] = layer
    stream = layer.astype(F32)
    scaled = (stream * gain_ref[...]).astype(BF)
    tokens, feats = stream.shape
    squares = lax.dot_general(
        jnp.ones((16, feats), F32), stream * stream, (((1,), (1,)), ((), ())),
        preferred_element_type=F32, precision=lax.Precision.HIGHEST,
    ).astype(BF)
    term = jnp.dot(scaled, weight_ref[...], preferred_element_type=F32).astype(BF)
    for block in range(tokens // BLK):
        for j in range(2 * KVH):
            at = block * 2 * KVH + j
            out_ref[at, :BLK, :] = term[block * BLK : (block + 1) * BLK, j * HEAD : (j + 1) * HEAD]
            out_ref[at, BLK:, :] = squares[:, block * BLK : (block + 1) * BLK]


def tile_kernel(parts_ref, tile_ref):
    total = jnp.sum(parts_ref[...].astype(F32), axis=0)
    scale = lax.rsqrt(total[BLK : BLK + 1, :] / D + EPS)
    column = jnp.transpose(jnp.broadcast_to(scale, (BLK, BLK)))
    tile_ref[...] = (total[:BLK, :] * column).astype(BF)


def invert(owner_ref, start_ref, count_ref, starts, counts):
    def one(r, carry):
        starts[owner_ref[r]] = start_ref[r]
        counts[owner_ref[r]] = count_ref[r]
        return carry

    lax.fori_loop(0, owner_ref.shape[0], one, 0)


def send_kernel(
    place_ref, owner_ref, start_ref, count_ref, own_ref, near_ref, mid_ref, far_ref,
    out_ref, held_ref, starts, counts,
):
    invert(owner_ref, start_ref, count_ref, starts, counts)
    place, parity = place_ref[0], place_ref[2]
    for back, ref in enumerate((own_ref, near_ref, mid_ref, far_ref)):
        held_ref[lax.rem(place + 4 - back, 4)] = ref[...]
    targets = out_ref.shape[0]

    def one(target, carry):
        first, count = starts[place * targets + target], counts[place * targets + target]
        slot = lax.rem(parity + first, 2)
        for k in range(2):
            at = slot + 2 * k
            holder = jnp.minimum((first + at) // 2, 3)
            tile = held_ref[holder]
            out_ref[target, k] = jnp.where(at < count, tile, jnp.zeros_like(tile))
        return carry

    lax.fori_loop(0, targets, one, 0)


def cache_kernel(place_ref, owner_ref, start_ref, arrived_ref, out_ref, starts, counts, sems):
    invert(owner_ref, start_ref, start_ref, starts, counts)
    odd = lax.rem(starts[place_ref[3]], 2)
    copies = []
    for half in range(2):
        slot = jnp.where(odd == 1, 1 - half, half)
        for k in range(2):
            copies.append(
                pltpu.make_async_copy(
                    arrived_ref.at[half, :, k], out_ref.at[slot + 2 * k], sems.at[half, k]
                )
            )
    for copy in copies:
        copy.start()
    for copy in copies:
        copy.wait()


def shape(dims, kind):
    return jax.ShapeDtypeStruct(dims, kind)


def per_device(
    conv_out,
    gate_in,
    residual,
    xproj_weight,
    dtproj_weight,
    dt_bias,
    a_log,
    d_skip,
    init_state,
    out_weight,
    norm_gain,
    kv_weight,
    owner,
    block_start,
    block_count,
):
    tp_count = lax.axis_size("tp")
    ctx_count = lax.axis_size("ctx")
    tokens, chans = conv_out.shape
    feats = residual.shape[1]
    pairs = tp_count // 2
    place = lax.axis_index("ctx")
    member = lax.axis_index("tp")
    places = jnp.stack(
        [place, member % 2, member // (tp_count // 2), place * tp_count + member]
    ).astype(jnp.int32)
    columns = DTR + 2 * STATE

    part = pl.pallas_call(
        project_kernel, out_shape=shape((tokens, columns), BF), name="project"
    )(conv_out, xproj_weight.T)
    shares = lax.all_to_all(
        part.reshape(tp_count, tokens // tp_count, columns), "tp", 0, 0, tiled=True
    )
    mine = jnp.sum(shares.astype(F32), axis=0).astype(BF)
    projected = lax.all_to_all(
        jnp.broadcast_to(mine[None], (tp_count,) + mine.shape), "tp", 0, 0, tiled=True
    ).reshape(tokens, columns)

    blocks = tokens // CHUNK
    step, states, ends = pl.pallas_call(
        first_kernel,
        out_shape=(
            shape((tokens, chans), F32),
            shape((blocks, 2 * STATE, CHUNK), F32),
            shape((STATE + 8, chans), F32),
        ),
        scratch_shapes=[pltpu.VMEM((tokens, 128), F32), pltpu.VMEM((tokens, chans), F32)],
        compiler_params=params(32),
        name="first",
    )(projected, dtproj_weight, dt_bias.reshape(1, chans), a_log, conv_out)
    earlier = [
        lax.ppermute(ends, "ctx", [(z, z + s) for z in range(ctx_count - s)])
        for s in range(1, ctx_count)
    ]
    keep, give = pl.pallas_call(
        second_kernel,
        in_specs=[SM] + [VM] * 10 + [ANY],
        out_shape=(shape((pairs, tokens, feats), BF),) * 2,
        scratch_shapes=[
            pltpu.VMEM((tokens, chans), F32),
            pltpu.VMEM((tokens, chans), F32),
            pltpu.VMEM((2, pairs, chans, feats), BF),
            pltpu.SemaphoreType.DMA((2, pairs)),
        ],
        compiler_params=params(40),
        name="second",
    )(
        places, step, states, a_log, conv_out, gate_in, d_skip.reshape(1, chans), init_state,
        *earlier, out_weight,
    )
    got = lax.ppermute(give, "tp", [(i, i ^ 1) for i in range(tp_count)])
    summed = (keep.astype(F32) + got.astype(F32)).astype(BF)
    groups = [[2 * i + c for i in range(pairs)] for c in range(2)]
    parts = lax.all_to_all(summed, "tp", 0, 0, axis_index_groups=groups, tiled=True)

    layer_out, kv_terms = pl.pallas_call(
        layer_kernel,
        out_shape=(shape((tokens, feats), BF), shape((tp_count, BLK + 16, HEAD), BF)),
        compiler_params=params(32),
        name="layer",
    )(parts, residual, norm_gain.reshape(1, feats), kv_weight)
    kv_parts = lax.all_to_all(kv_terms, "tp", 0, 0, tiled=True)
    tile = pl.pallas_call(
        tile_kernel, out_shape=shape((BLK, HEAD), BF), compiler_params=params(32), name="tile"
    )(kv_parts)
    others = [
        lax.ppermute(tile, "ctx", [(z, (z + s) % ctx_count) for z in range(ctx_count)])
        for s in range(1, ctx_count)
    ]
    devices = owner.shape[0]
    outgoing = pl.pallas_call(
        send_kernel,
        in_specs=[SM] * 4 + [VM] * 4,
        out_shape=shape((tp_count, 2, BLK, HEAD), BF),
        scratch_shapes=[
            pltpu.VMEM((ctx_count, BLK, HEAD), BF),
            pltpu.SMEM((devices,), jnp.int32),
            pltpu.SMEM((devices,), jnp.int32),
        ],
        compiler_params=params(32),
        name="send",
    )(places, owner, block_start, block_count, tile, *others)
    arrived = lax.all_to_all(outgoing, "tp", 0, 0, tiled=True)
    kv_cache = pl.pallas_call(
        cache_kernel,
        in_specs=[SM] * 3 + [ANY],
        out_specs=ANY,
        out_shape=shape((CAP, 2 * KVH, BLK, HEAD), BF),
        scratch_shapes=[
            pltpu.SMEM((devices,), jnp.int32),
            pltpu.SMEM((devices,), jnp.int32),
            pltpu.SemaphoreType.DMA((2, 2)),
        ],
        compiler_params=params(32),
        name="cache",
    )(places, owner, block_start, arrived.reshape(2, 2 * KVH, 2, BLK, HEAD))
    return (layer_out, kv_cache[None])


def solution(mesh):
    placed = (
        P("ctx", "tp"),
        P("ctx", "tp"),
        P("ctx", "tp"),
        P("tp", None),
        P(None, "tp"),
        P("tp"),
        P(None, "tp"),
        P("tp"),
        P(None, "tp"),
        P("tp", None),
        P("tp"),
        P("tp", None),
        P(),
        P(),
        P(),
    )
    return jax.shard_map(
        per_device,
        mesh=mesh,
        in_specs=placed,
        out_specs=(P("ctx", "tp"), P(("ctx", "tp"), None, None, None, None)),
        check_vma=False,
    )
```

```python
import jax
import jax.numpy as jnp
from jax import lax
from jax.experimental import pallas as pl
from jax.experimental.pallas import tpu as pltpu
from jax.sharding import PartitionSpec as P

D = 8192
STATE = 16
DTR = 512
KVH = 8
HEAD = 128
BLK = 128
CAP = 4
EPS = 1e-05
LOG2E = 1.4426950408889634
CHUNK = 32
PIECES = 8
BF = jnp.bfloat16
F32 = jnp.float32

VM = pl.BlockSpec(memory_space=pltpu.VMEM)
SM = pl.BlockSpec(memory_space=pltpu.SMEM)
ANY = pl.BlockSpec(memory_space=pl.ANY)


def params(mib):
    return pltpu.CompilerParams(vmem_limit_bytes=mib * 1024 * 1024)


def project_kernel(conv_ref, weight_ref, out_ref):
    out_ref[...] = lax.dot_general(
        conv_ref[...], weight_ref[...], (((1,), (1,)), ((), ())), preferred_element_type=F32
    ).astype(BF)


def advance_block(block, hidden, step_ref, drive_ref, states_ref, rates, read_out):
    states = states_ref[block]
    for group in range(CHUNK // 8):
        rows = pl.ds(pl.multiple_of(block * CHUNK + group * 8, 8), 8)
        steps, drives = step_ref[rows, :], drive_ref[rows, :]
        outs = []
        for i in range(8):
            at = group * 8 + i
            decay = jnp.exp2(steps[i : i + 1, :] * rates)
            hidden = decay * hidden + states[:STATE, at : at + 1] * drives[i : i + 1, :]
            if read_out is not None:
                outs.append(
                    jnp.sum(hidden * states[STATE:, at : at + 1], axis=0, keepdims=True)
                )
        if read_out is not None:
            read_out[rows, :] = jnp.concatenate(outs, axis=0)
    return hidden


def first_kernel(
    proj_ref, weight_ref, bias_ref, alog_ref, conv_ref,
    step_ref, states_ref, ends_ref, wide_ref, drive_ref,
):
    tokens = step_ref.shape[0]
    wide_ref[:, : 2 * STATE] = proj_ref[:, DTR:].astype(F32)
    flipped = jnp.transpose(wide_ref[...])
    for block in range(tokens // CHUNK):
        states_ref[block] = flipped[: 2 * STATE, block * CHUNK : (block + 1) * CHUNK]
    step = jax.nn.softplus(
        jnp.dot(proj_ref[:, :DTR], weight_ref[...], preferred_element_type=F32) + bias_ref[...]
    )
    step_ref[...] = step
    drive_ref[...] = step * conv_ref[...].astype(F32)
    rates = -jnp.exp(alog_ref[...]) * LOG2E
    hidden = lax.fori_loop(
        0,
        tokens // CHUNK,
        lambda k, h: advance_block(k, h, step_ref, drive_ref, states_ref, rates, None),
        jnp.zeros_like(rates),
    )
    ends_ref[:STATE, :] = hidden
    ends_ref[STATE:, :] = jnp.broadcast_to(jnp.sum(step, axis=0, keepdims=True), (8, step.shape[1]))


def give_kernel(
    place_ref, step_ref, states_ref, alog_ref, conv_ref, gate_ref, skip_ref, init_ref,
    near_ref, mid_ref, far_ref, weight_ref,
    give_ref, kept_ref, drive_ref, scan_ref, gated_ref, held_ref, sems,
):
    tokens = step_ref.shape[0]
    place, core = place_ref[0], place_ref[1]
    copies = fetch(weight_ref, held_ref, sems)
    rates = -jnp.exp(alog_ref[...]) * LOG2E
    hidden = init_ref[...]
    for back, ref in ((3, far_ref), (2, mid_ref), (1, near_ref)):
        passed = jnp.exp2(ref[STATE : STATE + 1, :] * rates) * hidden + ref[:STATE, :]
        hidden = jnp.where(place >= back, passed, hidden)
    drive_ref[...] = step_ref[...] * conv_ref[...].astype(F32)
    lax.fori_loop(
        0,
        tokens // CHUNK,
        lambda k, h: advance_block(k, h, step_ref, drive_ref, states_ref, rates, scan_ref),
        hidden,
    )
    gate = gate_ref[...].astype(F32)
    gated_ref[...] = (
        (scan_ref[...] + skip_ref[...] * conv_ref[...].astype(F32)) * (gate / (1.0 + jnp.exp(-gate)))
    ).astype(BF).reshape(gated_ref.shape)
    kept_ref[...] = gated_ref[core]
    through(gated_ref.at[1 - core], held_ref, copies, give_ref)


def fetch(weight_ref, held_ref, sems):
    wide = weight_ref.shape[1] // PIECES
    copies = [
        pltpu.make_async_copy(
            weight_ref.at[:, pl.ds(i * wide, wide)], held_ref.at[:, pl.ds(i * wide, wide)],
            sems.at[i],
        )
        for i in range(PIECES)
    ]
    for copy in copies:
        copy.start()
    return copies


def through(gated_ref, held_ref, copies, out_ref):
    chips, _, wide = out_ref.shape
    for chip in range(chips):
        if chip % (chips // PIECES) == 0:
            copies[chip // (chips // PIECES)].wait()
        out_ref[chip] = jnp.dot(
            gated_ref[...], held_ref[:, chip * wide : (chip + 1) * wide],
            preferred_element_type=F32,
        ).astype(BF)


def keep_kernel(kept_ref, weight_ref, keep_ref, held_ref, sems):
    through(kept_ref, held_ref, fetch(weight_ref, held_ref, sems), keep_ref)


def layer_kernel(
    place_ref, parts_ref, own_res_ref, got_res_ref, own_gain_ref, got_gain_ref,
    own_weight_ref, got_weight_ref, own_ref, other_ref, out_ref,
):
    mixed = jnp.sum(parts_ref[...].astype(F32), axis=0)
    half = mixed.shape[1] // 2
    first = place_ref[1] == 0
    left, right = mixed[:, :half], mixed[:, half:]
    term, squares = 0.0, 0.0
    for piece, res_ref, gain_ref, weight_ref, layer_ref in (
        (jnp.where(first, left, right), own_res_ref, own_gain_ref, own_weight_ref, own_ref),
        (jnp.where(first, right, left), got_res_ref, got_gain_ref, got_weight_ref, other_ref),
    ):
        layer = (res_ref[...].astype(F32) + piece).astype(BF)
        layer_ref[...] = layer
        stream = layer.astype(F32)
        squares = squares + lax.dot_general(
            jnp.ones((16, half), F32), stream * stream, (((1,), (1,)), ((), ())),
            preferred_element_type=F32, precision=lax.Precision.HIGHEST,
        )
        term = term + jnp.dot(
            (stream * gain_ref[...]).astype(BF), weight_ref[...], preferred_element_type=F32
        )
    term, squares = term.astype(BF), squares.astype(BF)
    for j in range(2 * KVH):
        out_ref[j, :BLK, :] = term[:, j * HEAD : (j + 1) * HEAD]
        out_ref[j, BLK:, :] = squares


def tile_kernel(parts_ref, tile_ref):
    total = jnp.sum(parts_ref[...].astype(F32), axis=0)
    scale = lax.rsqrt(total[BLK : BLK + 1, :] / D + EPS)
    column = jnp.transpose(jnp.broadcast_to(scale, (BLK, BLK)))
    tile_ref[...] = (total[:BLK, :] * column).astype(BF)


def send_kernel(
    place_ref, starts_ref, counts_ref, own_ref, near_ref, mid_ref, far_ref,
    own_layer_ref, got_layer_ref, out_ref, layer_ref, held_ref,
):
    place, core = place_ref[0], place_ref[1]
    for back, ref in enumerate((own_ref, near_ref, mid_ref, far_ref)):
        held_ref[lax.rem(place + 4 - back, 4)] = ref[...]
    for ref, half in ((own_layer_ref, core), (got_layer_ref, 1 - core)):
        rows = ref.shape[0]
        layer_ref[pl.ds(pl.multiple_of(half * rows, rows), rows), :] = ref[...]
    targets = out_ref.shape[0]

    def one(target, carry):
        first, count = starts_ref[place * targets + target], counts_ref[place * targets + target]
        slot = lax.rem(core + first, 2)
        for k in range(2):
            at = slot + 2 * k
            holder = jnp.minimum((first + at) // 2, 3)
            tile = held_ref[holder]
            out_ref[target, k] = jnp.where(at < count, tile, jnp.zeros_like(tile))
        return carry

    lax.fori_loop(0, targets, one, 0)


def cache_kernel(place_ref, starts_ref, arrived_ref, out_ref, sems):
    odd = lax.rem(starts_ref[place_ref[2]], 2)
    copies = []
    for half in range(2):
        slot = jnp.where(odd == 1, 1 - half, half)
        for k in range(2):
            copies.append(
                pltpu.make_async_copy(
                    arrived_ref.at[:, half, k], out_ref.at[slot + 2 * k], sems.at[half, k]
                )
            )
    for copy in copies:
        copy.start()
    for copy in copies:
        copy.wait()


def shape(dims, kind):
    return jax.ShapeDtypeStruct(dims, kind)


def per_device(
    conv_out,
    gate_in,
    residual,
    xproj_weight,
    dtproj_weight,
    dt_bias,
    a_log,
    d_skip,
    init_state,
    out_weight,
    norm_gain,
    kv_weight,
    owner,
    block_start,
    block_count,
):
    tp_count = lax.axis_size("tp")
    ctx_count = lax.axis_size("ctx")
    tokens, chans = conv_out.shape
    feats = residual.shape[1]
    pairs = tp_count // 2
    place = lax.axis_index("ctx")
    member = lax.axis_index("tp")
    core = member % 2
    places = jnp.stack([place, core, place * tp_count + member]).astype(jnp.int32)
    partner = [(i, i ^ 1) for i in range(tp_count)]

    def swap(value):
        return lax.ppermute(value, "tp", partner)

    halves = residual.reshape(2, tokens // 2, feats)
    own_res = lax.dynamic_index_in_dim(halves, core, 0, False)
    got_res = swap(lax.dynamic_index_in_dim(halves, 1 - core, 0, False))
    own_gain = norm_gain.reshape(1, feats)
    got_gain, got_weight = swap(own_gain), swap(kv_weight)
    devices = owner.shape[0]
    matches = owner[:, None] == jnp.arange(devices, dtype=jnp.int32)[None, :]
    starts = jnp.sum(jnp.where(matches, block_start[:, None], 0), axis=0)
    counts = jnp.sum(jnp.where(matches, block_count[:, None], 0), axis=0)
    columns = DTR + 2 * STATE

    part = pl.pallas_call(
        project_kernel, out_shape=shape((tokens, columns), BF), name="project"
    )(conv_out, xproj_weight.T)
    shares = lax.all_to_all(
        part.reshape(tp_count, tokens // tp_count, columns), "tp", 0, 0, tiled=True
    )
    shares, places, starts, counts, own_res, got_res, got_gain, got_weight = (
        lax.optimization_barrier(
            (shares, places, starts, counts, own_res, got_res, got_gain, got_weight)
        )
    )
    mine = jnp.sum(shares.astype(F32), axis=0).astype(BF)
    projected = lax.all_to_all(
        jnp.broadcast_to(mine[None], (tp_count,) + mine.shape), "tp", 0, 0, tiled=True
    ).reshape(tokens, columns)

    blocks = tokens // CHUNK
    step, states, ends = pl.pallas_call(
        first_kernel,
        out_shape=(
            shape((tokens, chans), F32),
            shape((blocks, 2 * STATE, CHUNK), F32),
            shape((STATE + 8, chans), F32),
        ),
        scratch_shapes=[pltpu.VMEM((tokens, 128), F32), pltpu.VMEM((tokens, chans), F32)],
        compiler_params=params(8),
        name="first",
    )(projected, dtproj_weight, dt_bias.reshape(1, chans), a_log, conv_out)
    def ranges_back(value):
        return [
            lax.ppermute(value, "ctx", [(z, (z + s) % ctx_count) for z in range(ctx_count)])
            for s in range(1, ctx_count)
        ]

    weight_scratch = [pltpu.VMEM(out_weight.shape, BF), pltpu.SemaphoreType.DMA((PIECES,))]
    partial = (pairs, tokens // 2, 2 * feats)
    give, kept = pl.pallas_call(
        give_kernel,
        in_specs=[SM] + [VM] * 10 + [ANY],
        out_shape=(shape(partial, BF), shape((tokens // 2, chans), BF)),
        scratch_shapes=[
            pltpu.VMEM((tokens, chans), F32),
            pltpu.VMEM((tokens, chans), F32),
            pltpu.VMEM((2, tokens // 2, chans), BF),
        ] + weight_scratch,
        compiler_params=params(46),
        name="give",
    )(
        places, step, states, a_log, conv_out, gate_in, d_skip.reshape(1, chans), init_state,
        *ranges_back(ends), out_weight,
    )
    got = swap(give)
    keep = pl.pallas_call(
        keep_kernel,
        in_specs=[VM, ANY],
        out_shape=shape(partial, BF),
        scratch_shapes=weight_scratch,
        compiler_params=params(46),
        name="keep",
    )(kept, out_weight)
    summed = (keep.astype(F32) + got.astype(F32)).astype(BF)
    groups = [[2 * i + c for i in range(pairs)] for c in range(2)]
    parts = lax.all_to_all(summed, "tp", 0, 0, axis_index_groups=groups, tiled=True)

    block_shape = shape((tokens // 2, feats), BF)
    own_layer, other_layer, kv_terms = pl.pallas_call(
        layer_kernel,
        in_specs=[SM] + [VM] * 7,
        out_shape=(block_shape, block_shape, shape((pairs, BLK + 16, HEAD), BF)),
        compiler_params=params(8),
        name="layer",
    )(places, parts, own_res, got_res, own_gain, got_gain, kv_weight, got_weight)
    got_layer = swap(other_layer)
    kv_parts = lax.all_to_all(kv_terms, "tp", 0, 0, axis_index_groups=groups, tiled=True)
    tile = pl.pallas_call(
        tile_kernel, out_shape=shape((BLK, HEAD), BF), compiler_params=params(8), name="tile"
    )(kv_parts)
    outgoing, layer_out = pl.pallas_call(
        send_kernel,
        in_specs=[SM] * 3 + [VM] * 6,
        out_shape=(shape((tp_count, 2, BLK, HEAD), BF), shape((tokens, feats), BF)),
        scratch_shapes=[pltpu.VMEM((ctx_count, BLK, HEAD), BF)],
        compiler_params=params(8),
        name="send",
    )(places, starts, counts, tile, *ranges_back(tile), own_layer, got_layer)
    arrived = lax.all_to_all(outgoing, "tp", 0, 0, tiled=True)
    kv_cache = pl.pallas_call(
        cache_kernel,
        in_specs=[SM] * 2 + [ANY],
        out_specs=ANY,
        out_shape=shape((CAP, 2 * KVH, BLK, HEAD), BF),
        scratch_shapes=[pltpu.SemaphoreType.DMA((2, 2))],
        compiler_params=params(8),
        name="cache",
    )(places, starts, arrived.reshape(2 * KVH, 2, 2, BLK, HEAD))
    return (layer_out, kv_cache[None])


def solution(mesh):
    placed = (
        P("ctx", "tp"),
        P("ctx", "tp"),
        P("ctx", "tp"),
        P("tp", None),
        P(None, "tp"),
        P("tp"),
        P(None, "tp"),
        P("tp"),
        P(None, "tp"),
        P("tp", None),
        P("tp"),
        P("tp", None),
        P(),
        P(),
        P(),
    )
    return jax.shard_map(
        per_device,
        mesh=mesh,
        in_specs=placed,
        out_specs=(P("ctx", "tp"), P(("ctx", "tp"), None, None, None, None)),
        check_vma=False,
    )
```

```python
import jax
import jax.numpy as jnp
from jax import lax
from jax.experimental import pallas as pl
from jax.experimental.pallas import tpu as pltpu
from jax.sharding import PartitionSpec as P

D = 8192
STATE = 16
DTR = 512
KVH = 8
HEAD = 128
BLK = 128
CAP = 4
EPS = 1e-05
LOG2E = 1.4426950408889634
CHUNK = 32
PIECES = 8
SIDE = 4
BF = jnp.bfloat16
F32 = jnp.float32

VM = pl.BlockSpec(memory_space=pltpu.VMEM)
SM = pl.BlockSpec(memory_space=pltpu.SMEM)
ANY = pl.BlockSpec(memory_space=pl.ANY)


def params(mib):
    return pltpu.CompilerParams(vmem_limit_bytes=mib * 1024 * 1024)


def project_kernel(place_ref, conv_ref, weight_ref, kept_ref, give_ref):
    rows = kept_ref.shape[0]
    for ref, half in ((give_ref, 1 - place_ref[1]), (kept_ref, place_ref[1])):
        ref[...] = lax.dot_general(
            conv_ref[pl.ds(pl.multiple_of(half * rows, rows), rows), :], weight_ref[...],
            (((1,), (1,)), ((), ())), preferred_element_type=F32,
        ).astype(ref.dtype)


def add_kernel(*refs):
    total = refs[0][...].astype(F32)
    for ref in refs[1:-1]:
        total = total + ref[...].astype(F32)
    refs[-1][...] = total.astype(refs[-1].dtype)


def advance_block(block, hidden, step_ref, drive_ref, states_ref, rates, read_out):
    states = states_ref[block]
    for group in range(CHUNK // 8):
        rows = pl.ds(pl.multiple_of(block * CHUNK + group * 8, 8), 8)
        steps, drives = step_ref[rows, :], drive_ref[rows, :]
        outs = []
        for i in range(8):
            at = group * 8 + i
            decay = jnp.exp2(steps[i : i + 1, :] * rates)
            hidden = decay * hidden + states[:STATE, at : at + 1] * drives[i : i + 1, :]
            if read_out is not None:
                outs.append(
                    jnp.sum(hidden * states[STATE:, at : at + 1], axis=0, keepdims=True)
                )
        if read_out is not None:
            read_out[rows, :] = jnp.concatenate(outs, axis=0)
    return hidden


def first_kernel(
    place_ref, own_proj_ref, got_proj_ref, weight_ref, bias_ref, alog_ref, conv_ref,
    step_ref, states_ref, ends_ref, proj_ref, wide_ref, drive_ref,
):
    for ref, half in ((own_proj_ref, place_ref[1]), (got_proj_ref, 1 - place_ref[1])):
        rows = ref.shape[0]
        proj_ref[pl.ds(pl.multiple_of(half * rows, rows), rows), :] = ref[...]
    tokens = step_ref.shape[0]
    wide_ref[:, : 2 * STATE] = proj_ref[:, DTR:].astype(F32)
    flipped = jnp.transpose(wide_ref[...])
    for block in range(tokens // CHUNK):
        states_ref[block] = flipped[: 2 * STATE, block * CHUNK : (block + 1) * CHUNK]
    step = jax.nn.softplus(
        jnp.dot(proj_ref[:, :DTR], weight_ref[...], preferred_element_type=F32) + bias_ref[...]
    )
    step_ref[...] = step
    drive_ref[...] = step * conv_ref[...].astype(F32)
    rates = -jnp.exp(alog_ref[...]) * LOG2E
    hidden = lax.fori_loop(
        0,
        tokens // CHUNK,
        lambda k, h: advance_block(k, h, step_ref, drive_ref, states_ref, rates, None),
        jnp.zeros_like(rates),
    )
    ends_ref[:STATE, :] = hidden
    ends_ref[STATE:, :] = jnp.broadcast_to(jnp.sum(step, axis=0, keepdims=True), (8, step.shape[1]))


def give_kernel(
    place_ref, step_ref, states_ref, alog_ref, conv_ref, gate_ref, skip_ref, init_ref,
    near_ref, mid_ref, far_ref, weight_ref,
    give_ref, kept_ref, drive_ref, scan_ref, gated_ref, held_ref, sems,
):
    tokens = step_ref.shape[0]
    place, core = place_ref[0], place_ref[1]
    copies = fetch(weight_ref, held_ref, sems)
    rates = -jnp.exp(alog_ref[...]) * LOG2E
    hidden = init_ref[...]
    for back, ref in ((3, far_ref), (2, mid_ref), (1, near_ref)):
        passed = jnp.exp2(ref[STATE : STATE + 1, :] * rates) * hidden + ref[:STATE, :]
        hidden = jnp.where(place >= back, passed, hidden)
    drive_ref[...] = step_ref[...] * conv_ref[...].astype(F32)
    lax.fori_loop(
        0,
        tokens // CHUNK,
        lambda k, h: advance_block(k, h, step_ref, drive_ref, states_ref, rates, scan_ref),
        hidden,
    )
    gate = gate_ref[...].astype(F32)
    gated_ref[...] = (
        (scan_ref[...] + skip_ref[...] * conv_ref[...].astype(F32)) * (gate / (1.0 + jnp.exp(-gate)))
    ).astype(BF).reshape(gated_ref.shape)
    kept_ref[...] = gated_ref[core]
    through(place_ref, 1 - core, gated_ref.at[1 - core], held_ref, copies, give_ref)


def fetch(weight_ref, held_ref, sems):
    wide = weight_ref.shape[1] // PIECES
    copies = [
        pltpu.make_async_copy(
            weight_ref.at[:, pl.ds(i * wide, wide)], held_ref.at[:, pl.ds(i * wide, wide)],
            sems.at[i],
        )
        for i in range(PIECES)
    ]
    for copy in copies:
        copy.start()
    return copies


def chip_order(place_ref, core, chip):
    away_x = lax.rem(chip // SIDE - place_ref[3] + SIDE, SIDE)
    away_y = lax.rem(chip % SIDE - place_ref[4] + SIDE, SIDE)
    return jnp.where(core == 0, away_x, away_y), jnp.where(core == 0, away_y, away_x)


def through(place_ref, core, gated_ref, held_ref, copies, out_ref):
    chips, _, wide = out_ref.shape
    for chip in range(chips):
        if chip % (chips // PIECES) == 0:
            copies[chip // (chips // PIECES)].wait()
        product = jnp.dot(
            gated_ref[...], held_ref[:, chip * wide : (chip + 1) * wide],
            preferred_element_type=F32,
        ).astype(BF)
        far, near = chip_order(place_ref, core, chip)
        out_ref[far * SIDE + near] = product


def keep_kernel(place_ref, kept_ref, weight_ref, keep_ref, held_ref, sems):
    copies = fetch(weight_ref, held_ref, sems)
    through(place_ref, place_ref[1], kept_ref, held_ref, copies, keep_ref)


def pair_kernel(keep_ref, got_ref, *out_refs):
    for shift, ref in enumerate(out_refs):
        rows = slice(shift * SIDE, (shift + 1) * SIDE)
        ref[...] = (keep_ref[rows].astype(F32) + got_ref[rows].astype(F32)).astype(BF)


def line_kernel(own_ref, one_ref, two_ref, three_ref, *out_refs):
    for shift, ref in enumerate(out_refs):
        total = own_ref[shift].astype(F32)
        for other in (one_ref, two_ref, three_ref):
            total = total + other[shift].astype(F32)
        ref[...] = total.astype(ref.dtype)


def layer_kernel(
    place_ref, own_part_ref, one_ref, two_ref, three_ref, own_res_ref, got_res_ref, own_gain_ref, got_gain_ref,
    own_weight_ref, got_weight_ref, own_ref, other_ref, *out_refs,
):
    mixed = own_part_ref[...]
    for ref in (one_ref, two_ref, three_ref):
        mixed = mixed + ref[...].astype(F32)
    half = mixed.shape[1] // 2
    first = place_ref[1] == 0
    left, right = mixed[:, :half], mixed[:, half:]
    term, squares = 0.0, 0.0
    for piece, res_ref, gain_ref, weight_ref, layer_ref in (
        (jnp.where(first, left, right), own_res_ref, own_gain_ref, own_weight_ref, own_ref),
        (jnp.where(first, right, left), got_res_ref, got_gain_ref, got_weight_ref, other_ref),
    ):
        layer = (res_ref[...].astype(F32) + piece).astype(BF)
        layer_ref[...] = layer
        stream = layer.astype(F32)
        squares = squares + lax.dot_general(
            jnp.ones((16, half), F32), stream * stream, (((1,), (1,)), ((), ())),
            preferred_element_type=F32, precision=lax.Precision.HIGHEST,
        )
        term = term + jnp.dot(
            (stream * gain_ref[...]).astype(BF), weight_ref[...], preferred_element_type=F32
        )
    term, squares = term.astype(BF), squares.astype(BF)
    for j in range(2 * KVH):
        far, _ = chip_order(place_ref, place_ref[1], j)
        second = jnp.where(place_ref[1] == 0, j % SIDE, j // SIDE)
        for shift, ref in enumerate(out_refs):

            @pl.when(far == shift)
            def _(ref=ref, second=second, j=j):
                ref[second, :BLK, :] = term[:, j * HEAD : (j + 1) * HEAD]
                ref[second, BLK:, :] = squares


def tile_kernel(
    place_ref, own_part_ref, one_ref, two_ref, three_ref, own_layer_ref, got_layer_ref,
    tile_ref, layer_ref,
):
    for ref, half in ((own_layer_ref, place_ref[1]), (got_layer_ref, 1 - place_ref[1])):
        rows = ref.shape[0]
        layer_ref[pl.ds(pl.multiple_of(half * rows, rows), rows), :] = ref[...]
    total = own_part_ref[...].astype(F32)
    for ref in (one_ref, two_ref, three_ref):
        total = total + ref[...].astype(F32)
    scale = lax.rsqrt(total[0, BLK : BLK + 1, :] / D + EPS)
    column = jnp.transpose(jnp.broadcast_to(scale, (BLK, BLK)))
    tile_ref[...] = (total[:, :BLK, :] * column[None]).astype(BF)


def choose(place_ref, target, starts_ref, counts_ref, sources, out_ref):
    core = place_ref[1]
    first, count = starts_ref[target], counts_ref[target]
    slot = lax.rem(core + first, 2)
    for far, ref in enumerate(sources):
        first_axis = lax.rem(jnp.where(core == 0, place_ref[3], place_ref[4]) + SIDE - far, SIDE)
        for second in range(SIDE):
            column = jnp.where(core == 0, first_axis * SIDE + second, second * SIDE + first_axis)
            for k in range(2):
                at = slot + 2 * k
                tile = ref[jnp.minimum((first + at) // 2, SIDE - 1), second]
                out_ref[k, column] = jnp.where(at < count, tile, jnp.zeros_like(tile))


def stack_kernel(place_ref, own_ref, near_ref, mid_ref, far_ref, out_ref):
    for back, ref in enumerate((own_ref, near_ref, mid_ref, far_ref)):
        out_ref[lax.rem(place_ref[0] + SIDE - back, SIDE)] = ref[...]


def pick_kernel(place_ref, starts_ref, counts_ref, q0, q1, q2, q3, out_ref):
    device = place_ref[2]
    partner = device + 1 - 2 * place_ref[1]
    choose(place_ref, partner, starts_ref, counts_ref, (q0, q1, q2, q3), out_ref)


def slot_copies(place_ref, starts_ref, parity, source_ref, cache_ref, sems):
    slot = lax.rem(parity + starts_ref[place_ref[2]], 2)
    return [
        pltpu.make_async_copy(source_ref.at[k], cache_ref.at[slot + 2 * k], sems.at[k])
        for k in range(2)
    ]


def own_kernel(
    place_ref, starts_ref, counts_ref, q0, q1, q2, q3, cache_ref, held_ref, sems
):
    core = place_ref[1]
    choose(place_ref, place_ref[2], starts_ref, counts_ref, (q0, q1, q2, q3), held_ref)
    copies = slot_copies(place_ref, starts_ref, core, held_ref, cache_ref, sems)
    for copy in copies:
        copy.start()
    for copy in copies:
        copy.wait()


def rest_kernel(place_ref, starts_ref, got_ref, _, cache_ref, sems):
    copies = slot_copies(place_ref, starts_ref, 1 - place_ref[1], got_ref, cache_ref, sems)
    for copy in copies:
        copy.start()
    for copy in copies:
        copy.wait()


def shape(dims, kind):
    return jax.ShapeDtypeStruct(dims, kind)


def per_device(
    conv_out,
    gate_in,
    residual,
    xproj_weight,
    dtproj_weight,
    dt_bias,
    a_log,
    d_skip,
    init_state,
    out_weight,
    norm_gain,
    kv_weight,
    owner,
    block_start,
    block_count,
):
    tp_count = lax.axis_size("tp")
    ctx_count = lax.axis_size("ctx")
    tokens, chans = conv_out.shape
    feats = residual.shape[1]
    pairs = tp_count // 2
    place = lax.axis_index("ctx")
    member = lax.axis_index("tp")
    core = member % 2
    places = jnp.stack(
        [
            place, core, place * tp_count + member,
            member // (2 * SIDE), (member // 2) % SIDE,
        ]
    ).astype(jnp.int32)
    partner = [(i, i ^ 1) for i in range(tp_count)]

    def line(stage, value_of):
        return [
            lax.ppermute(
                value_of(shift),
                "tp",
                [
                    (
                        (x * SIDE + y) * 2 + c,
                        ((x + shift) % SIDE * SIDE + y) * 2 + c
                        if c == stage
                        else (x * SIDE + (y + shift) % SIDE) * 2 + c,
                    )
                    for x in range(SIDE)
                    for y in range(SIDE)
                    for c in range(2)
                ],
            )
            for shift in range(1, SIDE)
        ]

    def swap(value):
        return lax.ppermute(value, "tp", partner)

    halves = residual.reshape(2, tokens // 2, feats)
    own_res = lax.dynamic_index_in_dim(halves, core, 0, False)
    got_res = swap(lax.dynamic_index_in_dim(halves, 1 - core, 0, False))
    own_gain = norm_gain.reshape(1, feats)
    got_gain, got_weight = swap(own_gain), swap(kv_weight)
    devices = owner.shape[0]
    matches = owner[:, None] == jnp.arange(devices, dtype=jnp.int32)[None, :]
    starts = jnp.sum(jnp.where(matches, block_start[:, None], 0), axis=0)
    counts = jnp.sum(jnp.where(matches, block_count[:, None], 0), axis=0)
    columns = DTR + 2 * STATE

    def add(name, kind, *values):
        return pl.pallas_call(
            add_kernel,
            out_shape=shape(values[0].shape, kind),
            compiler_params=params(8),
            name=name,
        )(*values)

    rows = (tokens // 2, columns)
    kept_share, give_share = pl.pallas_call(
        project_kernel,
        in_specs=[SM] + [VM] * 2,
        out_shape=(shape(rows, F32), shape(rows, BF)),
        compiler_params=params(8),
        name="project",
    )(places, conv_out, xproj_weight.T)
    chip = add("chip", BF, kept_share, swap(give_share))
    row = add("row", BF, chip, *line(0, lambda shift: chip))
    row, starts, counts, own_res, got_res, got_gain, got_weight = lax.optimization_barrier(
        (row, starts, counts, own_res, got_res, got_gain, got_weight)
    )
    own_proj = add("plane", BF, row, *line(1, lambda shift: row))

    blocks = tokens // CHUNK
    step, states, ends = pl.pallas_call(
        first_kernel,
        out_shape=(
            shape((tokens, chans), F32),
            shape((blocks, 2 * STATE, CHUNK), F32),
            shape((STATE + 8, chans), F32),
        ),
        in_specs=[SM] + [VM] * 6,
        scratch_shapes=[
            pltpu.VMEM((tokens, columns), BF),
            pltpu.VMEM((tokens, 128), F32),
            pltpu.VMEM((tokens, chans), F32),
        ],
        compiler_params=params(8),
        name="first",
    )(places, own_proj, swap(own_proj), dtproj_weight, dt_bias.reshape(1, chans), a_log, conv_out)
    def ranges_back(value):
        return [
            lax.ppermute(value, "ctx", [(z, (z + s) % ctx_count) for z in range(ctx_count)])
            for s in range(1, ctx_count)
        ]

    weight_scratch = [pltpu.VMEM(out_weight.shape, BF), pltpu.SemaphoreType.DMA((PIECES,))]
    partial = (pairs, tokens // 2, 2 * feats)
    give, kept = pl.pallas_call(
        give_kernel,
        in_specs=[SM] + [VM] * 10 + [ANY],
        out_shape=(shape(partial, BF), shape((tokens // 2, chans), BF)),
        scratch_shapes=[
            pltpu.VMEM((tokens, chans), F32),
            pltpu.VMEM((tokens, chans), F32),
            pltpu.VMEM((2, tokens // 2, chans), BF),
        ] + weight_scratch,
        compiler_params=params(46),
        name="give",
    )(
        places, step, states, a_log, conv_out, gate_in, d_skip.reshape(1, chans), init_state,
        *ranges_back(ends), out_weight,
    )
    got = swap(give)
    keep = pl.pallas_call(
        keep_kernel,
        in_specs=[SM, VM, ANY],
        out_shape=shape(partial, BF),
        scratch_shapes=weight_scratch,
        compiler_params=params(46),
        name="keep",
    )(places, kept, out_weight)
    quarter = shape((SIDE, tokens // 2, 2 * feats), BF)
    sums = pl.pallas_call(
        pair_kernel, out_shape=(quarter,) * SIDE, compiler_params=params(12), name="pair"
    )(keep, got)
    row = (tokens // 2, 2 * feats)
    parts = pl.pallas_call(
        line_kernel,
        out_shape=(shape(row, F32),) + (shape(row, BF),) * (SIDE - 1),
        compiler_params=params(12),
        name="line",
    )(sums[0], *line(0, lambda shift: sums[shift]))
    parts = [parts[0]] + line(1, lambda shift: parts[shift])

    block_shape = shape((tokens // 2, feats), BF)
    own_layer, other_layer, *kv_terms = pl.pallas_call(
        layer_kernel,
        in_specs=[SM] + [VM] * 10,
        out_shape=(block_shape,) * 2 + (shape((SIDE, BLK + 16, HEAD), BF),) * SIDE,
        compiler_params=params(8),
        name="layer",
    )(places, *parts, own_res, got_res, own_gain, got_gain, kv_weight, got_weight)
    got_layer = swap(other_layer)
    kv_row = add("kv", BF, kv_terms[0], *line(0, lambda shift: kv_terms[shift]))
    tile, layer_out = pl.pallas_call(
        tile_kernel,
        in_specs=[SM] + [VM] * 6,
        out_shape=(shape((SIDE, BLK, HEAD), BF), shape((tokens, feats), BF)),
        compiler_params=params(8),
        name="tile",
    )(places, kv_row, *line(1, lambda shift: kv_row), own_layer, got_layer)
    stacked = pl.pallas_call(
        stack_kernel,
        in_specs=[SM] + [VM] * 4,
        out_shape=shape((ctx_count, SIDE, BLK, HEAD), BF),
        compiler_params=params(4),
        name="stack",
    )(places, tile, *ranges_back(tile))
    everything = [stacked] + line(0, lambda shift: stacked)
    half_cache = shape((2, 2 * KVH, BLK, HEAD), BF)
    give_tiles = pl.pallas_call(
        pick_kernel,
        in_specs=[SM] * 3 + [VM] * SIDE,
        out_shape=half_cache,
        compiler_params=params(8),
        name="pick",
    )(places, starts, counts, *everything)
    got_tiles = swap(give_tiles)
    kv_cache = pl.pallas_call(
        own_kernel,
        in_specs=[SM] * 3 + [VM] * SIDE,
        out_specs=ANY,
        out_shape=shape((CAP, 2 * KVH, BLK, HEAD), BF),
        scratch_shapes=[pltpu.VMEM(half_cache.shape, BF), pltpu.SemaphoreType.DMA((2,))],
        compiler_params=params(8),
        name="own",
    )(places, starts, counts, *everything)
    kv_cache = pl.pallas_call(
        rest_kernel,
        in_specs=[SM] * 2 + [VM, ANY],
        out_specs=ANY,
        out_shape=shape((CAP, 2 * KVH, BLK, HEAD), BF),
        input_output_aliases={3: 0},
        scratch_shapes=[pltpu.SemaphoreType.DMA((2,))],
        compiler_params=params(4),
        name="rest",
    )(places, starts, got_tiles, kv_cache)
    return (layer_out, kv_cache[None])


def solution(mesh):
    placed = (
        P("ctx", "tp"),
        P("ctx", "tp"),
        P("ctx", "tp"),
        P("tp", None),
        P(None, "tp"),
        P("tp"),
        P(None, "tp"),
        P("tp"),
        P(None, "tp"),
        P("tp", None),
        P("tp"),
        P("tp", None),
        P(),
        P(),
        P(),
    )
    return jax.shard_map(
        per_device,
        mesh=mesh,
        in_specs=placed,
        out_specs=(P("ctx", "tp"), P(("ctx", "tp"), None, None, None, None)),
        check_vma=False,
    )
```

```python
import jax
import jax.numpy as jnp
from jax import lax
from jax.experimental import pallas as pl
from jax.experimental.pallas import tpu as pltpu
from jax.sharding import PartitionSpec as P

D = 8192
STATE = 16
DTR = 512
KVH = 8
HEAD = 128
BLK = 128
CAP = 4
EPS = 1e-05
LOG2E = 1.4426950408889634
CHUNK = 32
PIECES = 8
SIDE = 4
BF = jnp.bfloat16
F32 = jnp.float32

VM = pl.BlockSpec(memory_space=pltpu.VMEM)
SM = pl.BlockSpec(memory_space=pltpu.SMEM)
ANY = pl.BlockSpec(memory_space=pl.ANY)


def params(mib):
    return pltpu.CompilerParams(vmem_limit_bytes=mib * 1024 * 1024)


def project_kernel(place_ref, conv_ref, weight_ref, kept_ref, give_ref):
    rows = kept_ref.shape[0]
    for ref, half in ((give_ref, 1 - place_ref[1]), (kept_ref, place_ref[1])):
        ref[...] = lax.dot_general(
            conv_ref[pl.ds(pl.multiple_of(half * rows, rows), rows), :], weight_ref[...],
            (((1,), (1,)), ((), ())), preferred_element_type=F32,
        ).astype(ref.dtype)


def add_kernel(*refs):
    total = refs[0][...].astype(F32)
    for ref in refs[1:-1]:
        total = total + ref[...].astype(F32)
    refs[-1][...] = total.astype(refs[-1].dtype)


def advance_block(block, hidden, step_ref, drive_ref, states_ref, rates, read_out):
    states = states_ref[block]
    for group in range(CHUNK // 8):
        rows = pl.ds(pl.multiple_of(block * CHUNK + group * 8, 8), 8)
        steps, drives = step_ref[rows, :], drive_ref[rows, :]
        outs = []
        for i in range(8):
            at = group * 8 + i
            decay = jnp.exp2(steps[i : i + 1, :] * rates)
            hidden = decay * hidden + states[:STATE, at : at + 1] * drives[i : i + 1, :]
            if read_out is not None:
                outs.append(
                    jnp.sum(hidden * states[STATE:, at : at + 1], axis=0, keepdims=True)
                )
        if read_out is not None:
            read_out[rows, :] = jnp.concatenate(outs, axis=0)
    return hidden


def first_kernel(
    place_ref, own_proj_ref, got_proj_ref, weight_ref, bias_ref, alog_ref, conv_ref,
    step_ref, states_ref, ends_ref, proj_ref, wide_ref, drive_ref,
):
    for ref, half in ((own_proj_ref, place_ref[1]), (got_proj_ref, 1 - place_ref[1])):
        rows = ref.shape[0]
        proj_ref[pl.ds(pl.multiple_of(half * rows, rows), rows), :] = ref[...]
    tokens = step_ref.shape[0]
    wide_ref[:, : 2 * STATE] = proj_ref[:, DTR:].astype(F32)
    flipped = jnp.transpose(wide_ref[...])
    for block in range(tokens // CHUNK):
        states_ref[block] = flipped[: 2 * STATE, block * CHUNK : (block + 1) * CHUNK]
    step = jax.nn.softplus(
        jnp.dot(proj_ref[:, :DTR], weight_ref[...], preferred_element_type=F32) + bias_ref[...]
    )
    step_ref[...] = step
    drive_ref[...] = step * conv_ref[...].astype(F32)
    rates = -jnp.exp(alog_ref[...]) * LOG2E
    hidden = lax.fori_loop(
        0,
        tokens // CHUNK,
        lambda k, h: advance_block(k, h, step_ref, drive_ref, states_ref, rates, None),
        jnp.zeros_like(rates),
    )
    ends_ref[:STATE, :] = hidden
    ends_ref[STATE:, :] = jnp.broadcast_to(jnp.sum(step, axis=0, keepdims=True), (8, step.shape[1]))


def give_kernel(
    place_ref, step_ref, states_ref, alog_ref, conv_ref, gate_ref, skip_ref, init_ref,
    near_ref, mid_ref, far_ref, weight_ref, residual_ref,
    give_ref, kept_ref, drive_ref, scan_ref, gated_ref,
):
    tokens = step_ref.shape[0]
    place, core = place_ref[0], place_ref[1]
    rates = -jnp.exp(alog_ref[...]) * LOG2E
    hidden = init_ref[...]
    for back, ref in ((3, far_ref), (2, mid_ref), (1, near_ref)):
        passed = jnp.exp2(ref[STATE : STATE + 1, :] * rates) * hidden + ref[:STATE, :]
        hidden = jnp.where(place >= back, passed, hidden)
    drive_ref[...] = step_ref[...] * conv_ref[...].astype(F32)
    lax.fori_loop(
        0,
        tokens // CHUNK,
        lambda k, h: advance_block(k, h, step_ref, drive_ref, states_ref, rates, scan_ref),
        hidden,
    )
    gate = gate_ref[...].astype(F32)
    gated_ref[...] = (
        (scan_ref[...] + skip_ref[...] * conv_ref[...].astype(F32)) * (gate / (1.0 + jnp.exp(-gate)))
    ).astype(BF).reshape(gated_ref.shape)
    kept_ref[...] = gated_ref[core]
    through(place_ref, 1 - core, gated_ref.at[1 - core], weight_ref, give_ref)
    rows, feats = residual_ref.shape[0] // 2, residual_ref.shape[1]
    mine = pl.ds(pl.multiple_of(core * feats, feats), feats)
    other = residual_ref[pl.ds(pl.multiple_of((1 - core) * rows, rows), rows), :]
    give_ref[0, :, mine] = (give_ref[0, :, mine].astype(F32) + other.astype(F32)).astype(BF)


def bring_kernel(weight_ref, _, held_ref, sems):
    wide = weight_ref.shape[1] // PIECES
    copies = [
        pltpu.make_async_copy(
            weight_ref.at[:, pl.ds(i * wide, wide)], held_ref.at[:, pl.ds(i * wide, wide)],
            sems.at[i],
        )
        for i in range(PIECES)
    ]
    for copy in copies:
        copy.start()
    for copy in copies:
        copy.wait()


def chip_order(place_ref, core, chip):
    away_x = lax.rem(chip // SIDE - place_ref[3] + SIDE, SIDE)
    away_y = lax.rem(chip % SIDE - place_ref[4] + SIDE, SIDE)
    return jnp.where(core == 0, away_x, away_y), jnp.where(core == 0, away_y, away_x)


def through(place_ref, core, gated_ref, weight_ref, out_ref):
    chips, _, wide = out_ref.shape
    for chip in range(chips):
        product = jnp.dot(
            gated_ref[...], weight_ref[:, chip * wide : (chip + 1) * wide],
            preferred_element_type=F32,
        ).astype(BF)
        far, near = chip_order(place_ref, core, chip)
        out_ref[far * SIDE + near] = product


def keep_kernel(place_ref, kept_ref, weight_ref, keep_ref):
    through(place_ref, place_ref[1], kept_ref, weight_ref, keep_ref)


def pair_kernel(keep_ref, got_ref, *out_refs):
    for shift, ref in enumerate(out_refs):
        rows = slice(shift * SIDE, (shift + 1) * SIDE)
        ref[...] = (keep_ref[rows].astype(F32) + got_ref[rows].astype(F32)).astype(ref.dtype)


def line_kernel(own_ref, one_ref, two_ref, three_ref, *out_refs):
    for shift, ref in enumerate(out_refs):
        total = own_ref[shift].astype(F32)
        for other in (one_ref, two_ref, three_ref):
            total = total + other[shift].astype(F32)
        ref[...] = total.astype(ref.dtype)


def layer_kernel(
    place_ref, own_part_ref, one_ref, two_ref, three_ref, residual_ref, own_gain_ref,
    got_gain_ref, own_weight_ref, got_weight_ref, own_ref, other_ref, *out_refs,
):
    mixed = own_part_ref[...]
    for ref in (one_ref, two_ref, three_ref):
        mixed = mixed + ref[...].astype(F32)
    half = mixed.shape[1] // 2
    first = place_ref[1] == 0
    left, right = mixed[:, :half], mixed[:, half:]
    rows = mixed.shape[0]
    residual = residual_ref[pl.ds(pl.multiple_of(place_ref[1] * rows, rows), rows), :].astype(F32)
    term, squares = 0.0, 0.0
    for piece, gain_ref, weight_ref, layer_ref in (
        (jnp.where(first, left, right) + residual, own_gain_ref, own_weight_ref, own_ref),
        (jnp.where(first, right, left), got_gain_ref, got_weight_ref, other_ref),
    ):
        layer = piece.astype(BF)
        layer_ref[...] = layer
        stream = layer.astype(F32)
        squares = squares + lax.dot_general(
            jnp.ones((16, half), F32), stream * stream, (((1,), (1,)), ((), ())),
            preferred_element_type=F32, precision=lax.Precision.HIGHEST,
        )
        term = term + jnp.dot(
            (stream * gain_ref[...]).astype(BF), weight_ref[...], preferred_element_type=F32
        )
    term, squares = term.astype(BF), squares.astype(BF)
    for j in range(2 * KVH):
        far, _ = chip_order(place_ref, place_ref[1], j)
        second = jnp.where(place_ref[1] == 0, j % SIDE, j // SIDE)
        for shift, ref in enumerate(out_refs):

            @pl.when(far == shift)
            def _(ref=ref, second=second, j=j):
                ref[second, :BLK, :] = term[:, j * HEAD : (j + 1) * HEAD]
                ref[second, BLK:, :] = squares


def tile_kernel(
    place_ref, own_part_ref, one_ref, two_ref, three_ref, own_layer_ref, got_layer_ref,
    tile_ref, layer_ref,
):
    for ref, half in ((own_layer_ref, place_ref[1]), (got_layer_ref, 1 - place_ref[1])):
        rows = ref.shape[0]
        layer_ref[pl.ds(pl.multiple_of(half * rows, rows), rows), :] = ref[...]
    total = own_part_ref[...].astype(F32)
    for ref in (one_ref, two_ref, three_ref):
        total = total + ref[...].astype(F32)
    scale = lax.rsqrt(total[0, BLK : BLK + 1, :] / D + EPS)
    column = jnp.transpose(jnp.broadcast_to(scale, (BLK, BLK)))
    tile_ref[...] = (total[:, :BLK, :] * column[None]).astype(BF)


def choose(place_ref, target, starts_ref, counts_ref, sources, out_ref):
    core = place_ref[1]
    first, count = starts_ref[target], counts_ref[target]
    slot = lax.rem(core + first, 2)
    for far, ref in enumerate(sources):
        first_axis = lax.rem(jnp.where(core == 0, place_ref[3], place_ref[4]) + SIDE - far, SIDE)
        for second in range(SIDE):
            column = jnp.where(core == 0, first_axis * SIDE + second, second * SIDE + first_axis)
            for k in range(2):
                at = slot + 2 * k
                tile = ref[jnp.minimum((first + at) // 2, SIDE - 1), second]
                out_ref[k, column] = jnp.where(at < count, tile, jnp.zeros_like(tile))


def stack_kernel(place_ref, own_ref, near_ref, mid_ref, far_ref, out_ref):
    for back, ref in enumerate((own_ref, near_ref, mid_ref, far_ref)):
        out_ref[lax.rem(place_ref[0] + SIDE - back, SIDE)] = ref[...]


def pick_kernel(place_ref, starts_ref, counts_ref, q0, q1, q2, q3, out_ref):
    device = place_ref[2]
    partner = device + 1 - 2 * place_ref[1]
    choose(place_ref, partner, starts_ref, counts_ref, (q0, q1, q2, q3), out_ref)


def slot_copies(place_ref, starts_ref, parity, source_ref, cache_ref, sems):
    slot = lax.rem(parity + starts_ref[place_ref[2]], 2)
    return [
        pltpu.make_async_copy(source_ref.at[k], cache_ref.at[slot + 2 * k], sems.at[k])
        for k in range(2)
    ]


def own_kernel(
    place_ref, starts_ref, counts_ref, q0, q1, q2, q3, cache_ref, held_ref, sems
):
    core = place_ref[1]
    choose(place_ref, place_ref[2], starts_ref, counts_ref, (q0, q1, q2, q3), held_ref)
    copies = slot_copies(place_ref, starts_ref, core, held_ref, cache_ref, sems)
    for copy in copies:
        copy.start()
    for copy in copies:
        copy.wait()


def rest_kernel(place_ref, starts_ref, got_ref, _, cache_ref, sems):
    copies = slot_copies(place_ref, starts_ref, 1 - place_ref[1], got_ref, cache_ref, sems)
    for copy in copies:
        copy.start()
    for copy in copies:
        copy.wait()


def shape(dims, kind):
    return jax.ShapeDtypeStruct(dims, kind)


def per_device(
    conv_out,
    gate_in,
    residual,
    xproj_weight,
    dtproj_weight,
    dt_bias,
    a_log,
    d_skip,
    init_state,
    out_weight,
    norm_gain,
    kv_weight,
    owner,
    block_start,
    block_count,
):
    tp_count = lax.axis_size("tp")
    ctx_count = lax.axis_size("ctx")
    tokens, chans = conv_out.shape
    feats = residual.shape[1]
    pairs = tp_count // 2
    place = lax.axis_index("ctx")
    member = lax.axis_index("tp")
    core = member % 2
    places = jnp.stack(
        [
            place, core, place * tp_count + member,
            member // (2 * SIDE), (member // 2) % SIDE,
        ]
    ).astype(jnp.int32)
    partner = [(i, i ^ 1) for i in range(tp_count)]

    def line(stage, value_of):
        return [
            lax.ppermute(
                value_of(shift),
                "tp",
                [
                    (
                        (x * SIDE + y) * 2 + c,
                        ((x + shift) % SIDE * SIDE + y) * 2 + c
                        if c == stage
                        else (x * SIDE + (y + shift) % SIDE) * 2 + c,
                    )
                    for x in range(SIDE)
                    for y in range(SIDE)
                    for c in range(2)
                ],
            )
            for shift in range(1, SIDE)
        ]

    def swap(value):
        return lax.ppermute(value, "tp", partner)

    own_gain = norm_gain.reshape(1, feats)
    got_gain, got_weight = swap(own_gain), swap(kv_weight)
    devices = owner.shape[0]
    matches = owner[:, None] == jnp.arange(devices, dtype=jnp.int32)[None, :]
    starts = jnp.sum(jnp.where(matches, block_start[:, None], 0), axis=0)
    counts = jnp.sum(jnp.where(matches, block_count[:, None], 0), axis=0)
    columns = DTR + 2 * STATE

    def add(name, kind, *values):
        return pl.pallas_call(
            add_kernel,
            out_shape=shape(values[0].shape, kind),
            compiler_params=params(8),
            name=name,
        )(*values)

    rows = (tokens // 2, columns)
    kept_share, give_share = pl.pallas_call(
        project_kernel,
        in_specs=[SM] + [VM] * 2,
        out_shape=(shape(rows, F32), shape(rows, BF)),
        compiler_params=params(8),
        name="project",
    )(places, conv_out, xproj_weight.T)
    got_share, got_gain = lax.optimization_barrier((swap(give_share), got_gain))
    chip = add("chip", BF, kept_share, got_share)
    row = add("row", BF, chip, *line(0, lambda shift: chip))
    own_proj = add("plane", BF, row, *line(1, lambda shift: row))

    blocks = tokens // CHUNK
    step, states, ends = pl.pallas_call(
        first_kernel,
        out_shape=(
            shape((tokens, chans), F32),
            shape((blocks, 2 * STATE, CHUNK), F32),
            shape((STATE + 8, chans), F32),
        ),
        in_specs=[SM] + [VM] * 6,
        scratch_shapes=[
            pltpu.VMEM((tokens, columns), BF),
            pltpu.VMEM((tokens, 128), F32),
            pltpu.VMEM((tokens, chans), F32),
        ],
        compiler_params=params(8),
        name="first",
    )(places, own_proj, swap(own_proj), dtproj_weight, dt_bias.reshape(1, chans), a_log, conv_out)
    def ranges_back(value):
        return [
            lax.ppermute(value, "ctx", [(z, (z + s) % ctx_count) for z in range(ctx_count)])
            for s in range(1, ctx_count)
        ]

    near_weight = pl.pallas_call(
        bring_kernel,
        in_specs=[ANY] * 2,
        out_shape=shape(out_weight.shape, BF),
        scratch_shapes=[pltpu.SemaphoreType.DMA((PIECES,))],
        compiler_params=params(42),
        name="bring",
    )(out_weight, ends)
    partial = (pairs, tokens // 2, 2 * feats)
    give, kept = pl.pallas_call(
        give_kernel,
        in_specs=[SM] + [VM] * 12,
        out_shape=(shape(partial, BF), shape((tokens // 2, chans), BF)),
        scratch_shapes=[
            pltpu.VMEM((tokens, chans), F32),
            pltpu.VMEM((tokens, chans), F32),
            pltpu.VMEM((2, tokens // 2, chans), BF),
        ],
        compiler_params=params(20),
        name="give",
    )(
        places, step, states, a_log, conv_out, gate_in, d_skip.reshape(1, chans), init_state,
        *ranges_back(ends), near_weight, residual,
    )
    got = swap(give)
    keep = pl.pallas_call(
        keep_kernel,
        in_specs=[SM, VM, VM],
        out_shape=shape(partial, BF),
        compiler_params=params(16),
        name="keep",
    )(places, kept, near_weight)
    quarter = shape((SIDE, tokens // 2, 2 * feats), BF)
    sums = pl.pallas_call(
        pair_kernel, out_shape=(quarter,) * SIDE, compiler_params=params(12), name="pair"
    )(keep, got)
    row = (tokens // 2, 2 * feats)
    parts = pl.pallas_call(
        line_kernel,
        out_shape=(shape(row, F32),) + (shape(row, BF),) * (SIDE - 1),
        compiler_params=params(12),
        name="line",
    )(sums[0], *line(0, lambda shift: sums[shift]))
    parts = [parts[0]] + line(1, lambda shift: parts[shift])

    block_shape = shape((tokens // 2, feats), BF)
    own_layer, other_layer, *kv_terms = pl.pallas_call(
        layer_kernel,
        in_specs=[SM] + [VM] * 9,
        out_shape=(block_shape,) * 2 + (shape((SIDE, BLK + 16, HEAD), BF),) * SIDE,
        compiler_params=params(8),
        name="layer",
    )(places, *parts, residual, own_gain, got_gain, kv_weight, got_weight)
    got_layer = swap(other_layer)
    kv_row = add("kv", BF, kv_terms[0], *line(0, lambda shift: kv_terms[shift]))
    tile, layer_out = pl.pallas_call(
        tile_kernel,
        in_specs=[SM] + [VM] * 6,
        out_shape=(shape((SIDE, BLK, HEAD), BF), shape((tokens, feats), BF)),
        compiler_params=params(8),
        name="tile",
    )(places, kv_row, *line(1, lambda shift: kv_row), own_layer, got_layer)
    stacked = pl.pallas_call(
        stack_kernel,
        in_specs=[SM] + [VM] * 4,
        out_shape=shape((ctx_count, SIDE, BLK, HEAD), BF),
        compiler_params=params(4),
        name="stack",
    )(places, tile, *ranges_back(tile))
    everything = [stacked] + line(0, lambda shift: stacked)
    half_cache = shape((2, 2 * KVH, BLK, HEAD), BF)
    give_tiles = pl.pallas_call(
        pick_kernel,
        in_specs=[SM] * 3 + [VM] * SIDE,
        out_shape=half_cache,
        compiler_params=params(8),
        name="pick",
    )(places, starts, counts, *everything)
    got_tiles = swap(give_tiles)
    kv_cache = pl.pallas_call(
        own_kernel,
        in_specs=[SM] * 3 + [VM] * SIDE,
        out_specs=ANY,
        out_shape=shape((CAP, 2 * KVH, BLK, HEAD), BF),
        scratch_shapes=[pltpu.VMEM(half_cache.shape, BF), pltpu.SemaphoreType.DMA((2,))],
        compiler_params=params(8),
        name="own",
    )(places, starts, counts, *everything)
    kv_cache = pl.pallas_call(
        rest_kernel,
        in_specs=[SM] * 2 + [VM, ANY],
        out_specs=ANY,
        out_shape=shape((CAP, 2 * KVH, BLK, HEAD), BF),
        input_output_aliases={3: 0},
        scratch_shapes=[pltpu.SemaphoreType.DMA((2,))],
        compiler_params=params(4),
        name="rest",
    )(places, starts, got_tiles, kv_cache)
    return (layer_out, kv_cache[None])


def solution(mesh):
    placed = (
        P("ctx", "tp"),
        P("ctx", "tp"),
        P("ctx", "tp"),
        P("tp", None),
        P(None, "tp"),
        P("tp"),
        P(None, "tp"),
        P("tp"),
        P(None, "tp"),
        P("tp", None),
        P("tp"),
        P("tp", None),
        P(),
        P(),
        P(),
    )
    return jax.shard_map(
        per_device,
        mesh=mesh,
        in_specs=placed,
        out_specs=(P("ctx", "tp"), P(("ctx", "tp"), None, None, None, None)),
        check_vma=False,
    )
```

```python
import functools

import jax
import jax.numpy as jnp
from jax import lax
from jax.experimental import pallas as pl
from jax.experimental.pallas import tpu as pltpu
from jax.sharding import PartitionSpec as P

D = 8192
STATE = 16
DTR = 512
KVH = 8
HEAD = 128
BLK = 128
CAP = 4
EPS = 1e-05
LOG2E = 1.4426950408889634
CHUNK = 32
PIECES = 8
SIDE = 4
EARLY, LATE = 1, (2, 3)
BF = jnp.bfloat16
F32 = jnp.float32

VM = pl.BlockSpec(memory_space=pltpu.VMEM)
SM = pl.BlockSpec(memory_space=pltpu.SMEM)
ANY = pl.BlockSpec(memory_space=pl.ANY)


def params(mib):
    return pltpu.CompilerParams(vmem_limit_bytes=mib * 1024 * 1024)


def project_kernel(give, place_ref, conv_ref, weight_ref, out_ref):
    half = 1 - place_ref[1] if give else place_ref[1]
    conv = conv_ref[pl.ds(pl.multiple_of(half * BLK, BLK), BLK), :]
    both = (((1,), (1,)), ((), ()))
    out_ref[:BLK, :] = lax.dot_general(
        conv, weight_ref[:DTR, :], both, preferred_element_type=F32
    ).astype(out_ref.dtype)
    states = lax.dot_general(weight_ref[DTR:, :], conv, both, preferred_element_type=F32)
    packed = [states[i * 8 : (i + 1) * 8, :] for i in range(DTR // BLK)]
    packed = jnp.concatenate(packed, axis=1)
    out_ref[BLK:, :] = jnp.concatenate([packed, jnp.zeros_like(packed)], axis=0).astype(out_ref.dtype)


def add_kernel(*refs):
    total = refs[0][...].astype(F32)
    for ref in refs[1:-1]:
        total = total + ref[...].astype(F32)
    refs[-1][...] = total.astype(refs[-1].dtype)


def advance_block(block, hidden, step_ref, drive_ref, states_ref, rates, read_out):
    states = states_ref[block]
    for group in range(CHUNK // 8):
        rows = pl.ds(pl.multiple_of(block * CHUNK + group * 8, 8), 8)
        steps, drives = step_ref[rows, :], drive_ref[rows, :]
        outs = []
        for i in range(8):
            at = group * 8 + i
            decay = jnp.exp2(steps[i : i + 1, :] * rates)
            hidden = decay * hidden + states[:STATE, at : at + 1] * drives[i : i + 1, :]
            if read_out is not None:
                outs.append(
                    jnp.sum(hidden * states[STATE:, at : at + 1], axis=0, keepdims=True)
                )
        if read_out is not None:
            read_out[rows, :] = jnp.concatenate(outs, axis=0)
    return hidden


def first_kernel(
    place_ref, own_proj_ref, got_proj_ref, weight_ref, bias_ref, alog_ref, conv_ref,
    step_ref, states_ref, ends_ref, proj_ref, drive_ref,
):
    tokens = step_ref.shape[0]
    for ref, half in ((own_proj_ref, place_ref[1]), (got_proj_ref, 1 - place_ref[1])):
        proj_ref[pl.ds(pl.multiple_of(half * BLK, BLK), BLK), :] = ref[:BLK, :]
        packed = ref[BLK:, :].astype(F32)
        for group in range(DTR // BLK):
            for block in range(BLK // CHUNK):
                at = group * BLK + block * CHUNK
                states_ref[half * (BLK // CHUNK) + block, group * 8 : (group + 1) * 8, :] = (
                    packed[:8, at : at + CHUNK]
                )
    step = jax.nn.softplus(
        jnp.dot(proj_ref[...], weight_ref[...], preferred_element_type=F32) + bias_ref[...]
    )
    step_ref[...] = step
    drive_ref[...] = step * conv_ref[...].astype(F32)
    rates = -jnp.exp(alog_ref[...]) * LOG2E
    hidden = lax.fori_loop(
        0,
        tokens // CHUNK,
        lambda k, h: advance_block(k, h, step_ref, drive_ref, states_ref, rates, None),
        jnp.zeros_like(rates),
    )
    ends_ref[:STATE, :] = hidden
    ends_ref[STATE:, :] = jnp.broadcast_to(jnp.sum(step, axis=0, keepdims=True), (8, step.shape[1]))


def give_kernel(
    place_ref, step_ref, states_ref, alog_ref, conv_ref, gate_ref, skip_ref, init_ref,
    near_ref, mid_ref, far_ref, weight_ref, residual_ref,
    give_ref, kept_ref, drive_ref, scan_ref, gated_ref,
):
    tokens = step_ref.shape[0]
    place, core = place_ref[0], place_ref[1]
    rates = -jnp.exp(alog_ref[...]) * LOG2E
    hidden = init_ref[...]
    for back, ref in ((3, far_ref), (2, mid_ref), (1, near_ref)):
        passed = jnp.exp2(ref[STATE : STATE + 1, :] * rates) * hidden + ref[:STATE, :]
        hidden = jnp.where(place >= back, passed, hidden)
    drive_ref[...] = step_ref[...] * conv_ref[...].astype(F32)
    lax.fori_loop(
        0,
        tokens // CHUNK,
        lambda k, h: advance_block(k, h, step_ref, drive_ref, states_ref, rates, scan_ref),
        hidden,
    )
    gate = gate_ref[...].astype(F32)
    gated_ref[...] = (
        (scan_ref[...] + skip_ref[...] * conv_ref[...].astype(F32)) * (gate / (1.0 + jnp.exp(-gate)))
    ).astype(BF).reshape(gated_ref.shape)
    kept_ref[...] = gated_ref[core]
    through(place_ref, 1 - core, gated_ref.at[1 - core], weight_ref, give_ref)
    rows, feats = residual_ref.shape[0] // 2, residual_ref.shape[1]
    mine = pl.ds(pl.multiple_of(core * feats, feats), feats)
    other = residual_ref[pl.ds(pl.multiple_of((1 - core) * rows, rows), rows), :]
    give_ref[0, :, mine] = (give_ref[0, :, mine].astype(F32) + other.astype(F32)).astype(BF)


def bring_kernel(weight_ref, _, held_ref, sems):
    wide = weight_ref.shape[1] // PIECES
    copies = [
        pltpu.make_async_copy(
            weight_ref.at[:, pl.ds(i * wide, wide)], held_ref.at[:, pl.ds(i * wide, wide)],
            sems.at[i],
        )
        for i in range(PIECES)
    ]
    for copy in copies:
        copy.start()
    for copy in copies:
        copy.wait()


def chip_order(place_ref, core, chip):
    away_x = lax.rem(chip // SIDE - place_ref[3] + SIDE, SIDE)
    away_y = lax.rem(chip % SIDE - place_ref[4] + SIDE, SIDE)
    return jnp.where(core == 0, away_x, away_y), jnp.where(core == 0, away_y, away_x)


def through(place_ref, core, gated_ref, weight_ref, out_ref):
    chips, _, wide = out_ref.shape
    for chip in range(chips):
        product = jnp.dot(
            gated_ref[...], weight_ref[:, chip * wide : (chip + 1) * wide],
            preferred_element_type=F32,
        ).astype(BF)
        far, near = chip_order(place_ref, core, chip)
        out_ref[far * SIDE + near] = product


def keep_kernel(place_ref, kept_ref, weight_ref, keep_ref):
    through(place_ref, place_ref[1], kept_ref, weight_ref, keep_ref)


def pair_kernel(keep_ref, got_ref, *out_refs):
    for shift, ref in enumerate(out_refs):
        rows = slice(shift * SIDE, (shift + 1) * SIDE)
        ref[...] = (keep_ref[rows].astype(F32) + got_ref[rows].astype(F32)).astype(ref.dtype)


def line_kernel(own_ref, one_ref, two_ref, three_ref, *out_refs):
    for shift, ref in enumerate(out_refs):
        total = own_ref[shift].astype(F32)
        for other in (one_ref, two_ref, three_ref):
            total = total + other[shift].astype(F32)
        ref[...] = total.astype(ref.dtype)


def layer_kernel(
    place_ref, own_part_ref, one_ref, two_ref, three_ref, residual_ref, own_gain_ref,
    got_gain_ref, own_weight_ref, got_weight_ref, own_ref, other_ref, *rest,
):
    *out_refs, term_ref = rest
    mixed = own_part_ref[...]
    for ref in (one_ref, two_ref, three_ref):
        mixed = mixed + ref[...].astype(F32)
    half = mixed.shape[1] // 2
    first = place_ref[1] == 0
    left, right = mixed[:, :half], mixed[:, half:]
    rows = mixed.shape[0]
    residual = residual_ref[pl.ds(pl.multiple_of(place_ref[1] * rows, rows), rows), :].astype(F32)
    term, squares = 0.0, 0.0
    for piece, gain_ref, weight_ref, layer_ref in (
        (jnp.where(first, left, right) + residual, own_gain_ref, own_weight_ref, own_ref),
        (jnp.where(first, right, left), got_gain_ref, got_weight_ref, other_ref),
    ):
        layer = piece.astype(BF)
        layer_ref[...] = layer
        stream = layer.astype(F32)
        square = stream * stream
        upper = square.astype(BF)
        for value in (upper, (square - upper.astype(F32)).astype(BF)):
            squares = squares + lax.dot_general(
                jnp.ones((16, half), BF), value, (((1,), (1,)), ((), ())),
                preferred_element_type=F32,
            )
        term = term + jnp.dot(
            (stream * gain_ref[...]).astype(BF), weight_ref[...], preferred_element_type=F32
        )
    term_ref[...] = term.astype(BF)
    squares = squares.astype(BF)
    first_axis = jnp.where(first, place_ref[3], place_ref[4])
    for shift, ref in enumerate(out_refs):
        far = lax.rem(first_axis + shift, SIDE)
        for second in range(SIDE):
            j = jnp.where(first, far * SIDE + second, second * SIDE + far)
            ref[second, :BLK, :] = term_ref[:, pl.ds(pl.multiple_of(j * HEAD, HEAD), HEAD)]
            ref[second, BLK:, :] = squares


def tile_kernel(
    place_ref, own_part_ref, one_ref, two_ref, three_ref, own_layer_ref, got_layer_ref,
    tile_ref, layer_ref,
):
    for ref, half in ((own_layer_ref, place_ref[1]), (got_layer_ref, 1 - place_ref[1])):
        rows = ref.shape[0]
        layer_ref[pl.ds(pl.multiple_of(half * rows, rows), rows), :] = ref[...]
    total = own_part_ref[...].astype(F32)
    for ref in (one_ref, two_ref, three_ref):
        total = total + ref[...].astype(F32)
    scale = lax.rsqrt(total[0, BLK : BLK + 1, :] / D + EPS)
    column = jnp.transpose(jnp.broadcast_to(scale, (BLK, BLK)))
    tile_ref[...] = (total[:, :BLK, :] * column[None]).astype(BF)


def choose(place_ref, target, starts_ref, counts_ref, sources, out_ref):
    first, count = starts_ref[target], counts_ref[target]
    slot = lax.rem(place_ref[1] + first, 2)
    for i, ref in enumerate(sources):
        for second in range(SIDE):
            for k in range(2):
                at = slot + 2 * k
                tile = ref[jnp.minimum((first + at) // 2, SIDE - 1), second]
                out_ref[k, i * SIDE + second] = jnp.where(at < count, tile, jnp.zeros_like(tile))


def to_cache(place_ref, starts_ref, core, source_refs, cache_ref, sems):
    slot = lax.rem(core + starts_ref[place_ref[2]], 2)
    waits = []
    for i, shift in enumerate((0, EARLY, *LATE)):
        source_ref = source_refs[i // (SIDE // len(source_refs))]
        first_axis = lax.rem(jnp.where(core == 0, place_ref[3], place_ref[4]) + SIDE - shift, SIDE)
        at = i * SIDE % source_ref.shape[1]
        for k in range(2):
            part = source_ref.at[k, pl.ds(at, SIDE)]
            along_y = pltpu.make_async_copy(
                part, cache_ref.at[slot + 2 * k, first_axis], sems.at[k, i]
            )
            along_x = pltpu.make_async_copy(
                part, cache_ref.at[slot + 2 * k, :, first_axis], sems.at[k, i]
            )
            pl.when(core == 0)(along_y.start)
            pl.when(core == 1)(along_x.start)
            waits.append(along_y)
    for copy in waits:
        copy.wait()


def stack_kernel(place_ref, own_ref, near_ref, mid_ref, far_ref, out_ref):
    for back, ref in enumerate((own_ref, near_ref, mid_ref, far_ref)):
        out_ref[lax.rem(place_ref[0] + SIDE - back, SIDE)] = ref[...]


def pick_kernel(place_ref, starts_ref, counts_ref, one_ref, two_ref, out_ref):
    partner = place_ref[2] + 1 - 2 * place_ref[1]
    choose(place_ref, partner, starts_ref, counts_ref, (one_ref, two_ref), out_ref)


def own_kernel(place_ref, starts_ref, counts_ref, q0, q1, q2, q3, cache_ref, held_ref, sems):
    choose(place_ref, place_ref[2], starts_ref, counts_ref, (q0, q1, q2, q3), held_ref)
    to_cache(place_ref, starts_ref, place_ref[1], (held_ref,), cache_ref, sems)


def rest_kernel(place_ref, starts_ref, one_ref, two_ref, _, cache_ref, sems):
    to_cache(place_ref, starts_ref, 1 - place_ref[1], (one_ref, two_ref), cache_ref, sems)


def shape(dims, kind):
    return jax.ShapeDtypeStruct(dims, kind)


def per_device(
    conv_out,
    gate_in,
    residual,
    xproj_weight,
    dtproj_weight,
    dt_bias,
    a_log,
    d_skip,
    init_state,
    out_weight,
    norm_gain,
    kv_weight,
    owner,
    block_start,
    block_count,
):
    tp_count = lax.axis_size("tp")
    ctx_count = lax.axis_size("ctx")
    tokens, chans = conv_out.shape
    feats = residual.shape[1]
    pairs = tp_count // 2
    place = lax.axis_index("ctx")
    member = lax.axis_index("tp")
    core = member % 2
    places = jnp.stack(
        [
            place, core, place * tp_count + member,
            member // (2 * SIDE), (member // 2) % SIDE,
        ]
    ).astype(jnp.int32)
    partner = [(i, i ^ 1) for i in range(tp_count)]

    def line(stage, value_of):
        return [
            lax.ppermute(
                value_of(shift),
                "tp",
                [
                    (
                        (x * SIDE + y) * 2 + c,
                        ((x + shift) % SIDE * SIDE + y) * 2 + c
                        if c == stage
                        else (x * SIDE + (y + shift) % SIDE) * 2 + c,
                    )
                    for x in range(SIDE)
                    for y in range(SIDE)
                    for c in range(2)
                ],
            )
            for shift in range(1, SIDE)
        ]

    def swap(value):
        return lax.ppermute(value, "tp", partner)

    own_gain = norm_gain.reshape(1, feats)
    got_gain, got_weight = swap(own_gain), swap(kv_weight)
    devices = owner.shape[0]
    matches = owner[:, None] == jnp.arange(devices, dtype=jnp.int32)[None, :]
    starts = jnp.sum(jnp.where(matches, block_start[:, None], 0), axis=0)
    counts = jnp.sum(jnp.where(matches, block_count[:, None], 0), axis=0)

    def add(name, kind, *values):
        return pl.pallas_call(
            add_kernel,
            out_shape=shape(values[0].shape, kind),
            compiler_params=params(8),
            name=name,
        )(*values)

    def project(name, give, kind):
        return pl.pallas_call(
            functools.partial(project_kernel, give),
            in_specs=[SM] + [VM] * 2,
            out_shape=shape((BLK + 16, DTR), kind),
            compiler_params=params(8),
            name=name,
        )(places, conv_out, xproj_weight.T)

    give_share = project("project_give", True, BF)
    kept_share = project("project_keep", False, F32)
    got_share, got_gain = lax.optimization_barrier((swap(give_share), got_gain))
    chip = add("chip", BF, kept_share, got_share)
    row = add("row", BF, chip, *line(0, lambda shift: chip))
    own_proj = add("plane", BF, row, *line(1, lambda shift: row))

    blocks = tokens // CHUNK
    step, states, ends = pl.pallas_call(
        first_kernel,
        out_shape=(
            shape((tokens, chans), F32),
            shape((blocks, 2 * STATE, CHUNK), F32),
            shape((STATE + 8, chans), F32),
        ),
        in_specs=[SM] + [VM] * 6,
        scratch_shapes=[
            pltpu.VMEM((tokens, DTR), BF),
            pltpu.VMEM((tokens, chans), F32),
        ],
        compiler_params=params(8),
        name="first",
    )(places, own_proj, swap(own_proj), dtproj_weight, dt_bias.reshape(1, chans), a_log, conv_out)
    def ranges_back(value):
        return [
            lax.ppermute(value, "ctx", [(z, (z + s) % ctx_count) for z in range(ctx_count)])
            for s in range(1, ctx_count)
        ]

    near_weight = pl.pallas_call(
        bring_kernel,
        in_specs=[ANY] * 2,
        out_shape=shape(out_weight.shape, BF),
        scratch_shapes=[pltpu.SemaphoreType.DMA((PIECES,))],
        compiler_params=params(42),
        name="bring",
    )(out_weight, ends)
    partial = (pairs, tokens // 2, 2 * feats)
    give, kept = pl.pallas_call(
        give_kernel,
        in_specs=[SM] + [VM] * 12,
        out_shape=(shape(partial, BF), shape((tokens // 2, chans), BF)),
        scratch_shapes=[
            pltpu.VMEM((tokens, chans), F32),
            pltpu.VMEM((tokens, chans), F32),
            pltpu.VMEM((2, tokens // 2, chans), BF),
        ],
        compiler_params=params(20),
        name="give",
    )(
        places, step, states, a_log, conv_out, gate_in, d_skip.reshape(1, chans), init_state,
        *ranges_back(ends), near_weight, residual,
    )
    got = swap(give)
    keep = pl.pallas_call(
        keep_kernel,
        in_specs=[SM, VM, VM],
        out_shape=shape(partial, BF),
        compiler_params=params(16),
        name="keep",
    )(places, kept, near_weight)
    quarter = shape((SIDE, tokens // 2, 2 * feats), BF)
    sums = pl.pallas_call(
        pair_kernel, out_shape=(quarter,) * SIDE, compiler_params=params(12), name="pair"
    )(keep, got)
    row = (tokens // 2, 2 * feats)
    parts = pl.pallas_call(
        line_kernel,
        out_shape=(shape(row, F32),) + (shape(row, BF),) * (SIDE - 1),
        compiler_params=params(12),
        name="line",
    )(sums[0], *line(0, lambda shift: sums[shift]))
    parts = [parts[0]] + line(1, lambda shift: parts[shift])

    block_shape = shape((tokens // 2, feats), BF)
    own_layer, other_layer, *kv_terms = pl.pallas_call(
        layer_kernel,
        in_specs=[SM] + [VM] * 9,
        out_shape=(block_shape,) * 2 + (shape((SIDE, BLK + 16, HEAD), BF),) * SIDE,
        scratch_shapes=[pltpu.VMEM((tokens // 2, 2 * KVH * HEAD), BF)],
        compiler_params=params(8),
        name="layer",
    )(places, *parts, residual, own_gain, got_gain, kv_weight, got_weight)
    got_layer = swap(other_layer)
    kv_row = add("kv", BF, kv_terms[0], *line(0, lambda shift: kv_terms[shift]))
    tile, layer_out = pl.pallas_call(
        tile_kernel,
        in_specs=[SM] + [VM] * 6,
        out_shape=(shape((SIDE, BLK, HEAD), BF), shape((tokens, feats), BF)),
        compiler_params=params(8),
        name="tile",
    )(places, kv_row, *line(1, lambda shift: kv_row), own_layer, got_layer)
    stacked = pl.pallas_call(
        stack_kernel,
        in_specs=[SM] + [VM] * 4,
        out_shape=shape((ctx_count, SIDE, BLK, HEAD), BF),
        compiler_params=params(4),
        name="stack",
    )(places, tile, *ranges_back(tile))
    everything = [stacked] + line(0, lambda shift: stacked)
    chosen = (2, 2 * SIDE, BLK, HEAD)
    sems = pltpu.SemaphoreType.DMA((2, SIDE))
    cache_shape = shape((CAP, SIDE, SIDE, BLK, HEAD), BF)

    def for_partner(name, *sources):
        return swap(
            pl.pallas_call(
                pick_kernel,
                in_specs=[SM] * 3 + [VM] * 2,
                out_shape=shape(chosen, BF),
                compiler_params=params(4),
                name=name,
            )(places, starts, counts, *sources)
        )

    got_first = for_partner("pick0", everything[0], everything[EARLY])
    *late, got_first = lax.optimization_barrier((*[everything[i] for i in LATE], got_first))
    everything = [everything[0], everything[EARLY], *late]
    got_last = for_partner("pick1", *late)
    kv_cache = pl.pallas_call(
        own_kernel,
        in_specs=[SM] * 3 + [VM] * SIDE,
        out_specs=ANY,
        out_shape=cache_shape,
        scratch_shapes=[pltpu.VMEM((2, 4 * SIDE, BLK, HEAD), BF), sems],
        compiler_params=params(8),
        name="own",
    )(places, starts, counts, *everything)
    kv_cache = pl.pallas_call(
        rest_kernel,
        in_specs=[SM] * 2 + [VM, VM, ANY],
        out_specs=ANY,
        out_shape=cache_shape,
        input_output_aliases={4: 0},
        scratch_shapes=[sems],
        compiler_params=params(4),
        name="rest",
    )(places, starts, got_first, got_last, kv_cache)
    return (layer_out, kv_cache.reshape(1, CAP, 2 * KVH, BLK, HEAD))


def solution(mesh):
    placed = (
        P("ctx", "tp"),
        P("ctx", "tp"),
        P("ctx", "tp"),
        P("tp", None),
        P(None, "tp"),
        P("tp"),
        P(None, "tp"),
        P("tp"),
        P(None, "tp"),
        P("tp", None),
        P("tp"),
        P("tp", None),
        P(),
        P(),
        P(),
    )
    return jax.shard_map(
        per_device,
        mesh=mesh,
        in_specs=placed,
        out_specs=(P("ctx", "tp"), P(("ctx", "tp"), None, None, None, None)),
        check_vma=False,
    )
```

```python
import functools

import jax
import jax.numpy as jnp
from jax import lax
from jax.experimental import pallas as pl
from jax.experimental.pallas import tpu as pltpu
from jax.sharding import PartitionSpec as P

D = 8192
STATE = 16
DTR = 512
KVH = 8
HEAD = 128
BLK = 128
CAP = 4
EPS = 1e-05
LOG2E = 1.4426950408889634
CHUNK = 64
PIECES = 8
SIDE = 4
EARLY, LATE = 1, (2, 3)
BF = jnp.bfloat16
F32 = jnp.float32

VM = pl.BlockSpec(memory_space=pltpu.VMEM)
SM = pl.BlockSpec(memory_space=pltpu.SMEM)
ANY = pl.BlockSpec(memory_space=pl.ANY)


def params(mib):
    return pltpu.CompilerParams(vmem_limit_bytes=mib * 1024 * 1024)


def project_kernel(give, place_ref, conv_ref, weight_ref, out_ref):
    half = 1 - place_ref[1] if give else place_ref[1]
    conv = conv_ref[pl.ds(pl.multiple_of(half * BLK, BLK), BLK), :]
    both = (((1,), (1,)), ((), ()))
    out_ref[:BLK, :] = lax.dot_general(
        conv, weight_ref[:DTR, :], both, preferred_element_type=F32
    ).astype(out_ref.dtype)
    states = lax.dot_general(weight_ref[DTR:, :], conv, both, preferred_element_type=F32)
    packed = [states[i * 8 : (i + 1) * 8, :] for i in range(DTR // BLK)]
    packed = jnp.concatenate(packed, axis=1)
    out_ref[BLK:, :] = jnp.concatenate([packed, jnp.zeros_like(packed)], axis=0).astype(out_ref.dtype)


def add_kernel(*refs):
    total = refs[0][...].astype(F32)
    for ref in refs[1:-1]:
        total = total + ref[...].astype(F32)
    refs[-1][...] = total.astype(refs[-1].dtype)


def fold_rows(values):
    row = lax.broadcasted_iota(jnp.int32, values[0].shape, 0)
    for reach in (4, 2, 1):
        near = row % (2 * reach) < reach
        values = [
            jnp.where(near, a, b)
            + jnp.where(near, pltpu.roll(a, 8 - reach, 0), pltpu.roll(b, reach, 0))
            for a, b in zip(values[:reach], values[reach:], strict=True)
        ]
    return values[0]


def advance_block(block, hidden, step_ref, drive_ref, states_ref, rates, read_out):
    states = states_ref[block]
    for group in range(CHUNK // 8):
        rows = pl.ds(pl.multiple_of(block * CHUNK + group * 8, 8), 8)
        steps, drives = step_ref[rows, :], drive_ref[rows, :]
        outs = []
        for i in range(8):
            at = group * 8 + i
            decay = jnp.exp2(steps[i : i + 1, :] * rates)
            hidden = decay * hidden + states[:STATE, at : at + 1] * drives[i : i + 1, :]
            if read_out is not None:
                terms = hidden * states[STATE:, at : at + 1]
                outs.append(terms[:8] + terms[8:])
        if read_out is not None:
            read_out[rows, :] = fold_rows(outs)
    return hidden


def first_kernel(
    place_ref, own_proj_ref, got_proj_ref, weight_ref, bias_ref, alog_ref, conv_ref,
    step_ref, states_ref, ends_ref, proj_ref, drive_ref,
):
    tokens = step_ref.shape[0]
    for ref, half in ((own_proj_ref, place_ref[1]), (got_proj_ref, 1 - place_ref[1])):
        proj_ref[pl.ds(pl.multiple_of(half * BLK, BLK), BLK), :] = ref[:BLK, :]
        packed = ref[BLK:, :].astype(F32)
        for group in range(DTR // BLK):
            for block in range(BLK // CHUNK):
                at = group * BLK + block * CHUNK
                states_ref[half * (BLK // CHUNK) + block, group * 8 : (group + 1) * 8, :] = (
                    packed[:8, at : at + CHUNK]
                )
    step = jax.nn.softplus(
        jnp.dot(proj_ref[...], weight_ref[...], preferred_element_type=F32) + bias_ref[...]
    )
    step_ref[...] = step
    drive_ref[...] = step * conv_ref[...].astype(F32)
    rates = -jnp.exp(alog_ref[...]) * LOG2E
    hidden = lax.fori_loop(
        0,
        tokens // CHUNK,
        lambda k, h: advance_block(k, h, step_ref, drive_ref, states_ref, rates, None),
        jnp.zeros_like(rates),
    )
    ends_ref[:STATE, :] = hidden
    ends_ref[STATE:, :] = jnp.broadcast_to(jnp.sum(step, axis=0, keepdims=True), (8, step.shape[1]))


def give_kernel(
    place_ref, step_ref, states_ref, alog_ref, conv_ref, gate_ref, skip_ref, init_ref,
    near_ref, mid_ref, far_ref, weight_ref, residual_ref,
    give_ref, kept_ref, drive_ref, scan_ref, gated_ref,
):
    tokens = step_ref.shape[0]
    place, core = place_ref[0], place_ref[1]
    rates = -jnp.exp(alog_ref[...]) * LOG2E
    hidden = init_ref[...]
    for back, ref in ((3, far_ref), (2, mid_ref), (1, near_ref)):
        passed = jnp.exp2(ref[STATE : STATE + 1, :] * rates) * hidden + ref[:STATE, :]
        hidden = jnp.where(place >= back, passed, hidden)
    drive_ref[...] = step_ref[...] * conv_ref[...].astype(F32)
    lax.fori_loop(
        0,
        tokens // CHUNK,
        lambda k, h: advance_block(k, h, step_ref, drive_ref, states_ref, rates, scan_ref),
        hidden,
    )
    gate = gate_ref[...].astype(F32)
    gated_ref[...] = (
        (scan_ref[...] + skip_ref[...] * conv_ref[...].astype(F32)) * (gate / (1.0 + jnp.exp(-gate)))
    ).astype(BF).reshape(gated_ref.shape)
    kept_ref[...] = gated_ref[core]
    through(place_ref, 1 - core, gated_ref.at[1 - core], weight_ref, give_ref)
    rows, feats = residual_ref.shape[0] // 2, residual_ref.shape[1]
    mine = pl.ds(pl.multiple_of(core * feats, feats), feats)
    other = residual_ref[pl.ds(pl.multiple_of((1 - core) * rows, rows), rows), :]
    give_ref[0, :, mine] = (give_ref[0, :, mine].astype(F32) + other.astype(F32)).astype(BF)


def bring_kernel(weight_ref, _, held_ref, sems):
    wide = weight_ref.shape[1] // PIECES
    copies = [
        pltpu.make_async_copy(
            weight_ref.at[:, pl.ds(i * wide, wide)], held_ref.at[:, pl.ds(i * wide, wide)],
            sems.at[i],
        )
        for i in range(PIECES)
    ]
    for copy in copies:
        copy.start()
    for copy in copies:
        copy.wait()


def chip_order(place_ref, core, chip):
    away_x = lax.rem(chip // SIDE - place_ref[3] + SIDE, SIDE)
    away_y = lax.rem(chip % SIDE - place_ref[4] + SIDE, SIDE)
    return jnp.where(core == 0, away_x, away_y), jnp.where(core == 0, away_y, away_x)


def through(place_ref, core, gated_ref, weight_ref, out_ref):
    chips, _, wide = out_ref.shape
    for chip in range(chips):
        product = jnp.dot(
            gated_ref[...], weight_ref[:, chip * wide : (chip + 1) * wide],
            preferred_element_type=F32,
        ).astype(BF)
        far, near = chip_order(place_ref, core, chip)
        out_ref[far * SIDE + near] = product


def keep_kernel(place_ref, kept_ref, weight_ref, keep_ref):
    through(place_ref, place_ref[1], kept_ref, weight_ref, keep_ref)


def pair_kernel(keep_ref, got_ref, *out_refs):
    for shift, ref in enumerate(out_refs):
        rows = slice(shift * SIDE, (shift + 1) * SIDE)
        ref[...] = (keep_ref[rows].astype(F32) + got_ref[rows].astype(F32)).astype(ref.dtype)


def line_kernel(own_ref, one_ref, two_ref, three_ref, *out_refs):
    for shift, ref in enumerate(out_refs):
        total = own_ref[shift].astype(F32)
        for other in (one_ref, two_ref, three_ref):
            total = total + other[shift].astype(F32)
        ref[...] = total.astype(ref.dtype)


def layer_kernel(
    place_ref, own_part_ref, one_ref, two_ref, three_ref, residual_ref, own_gain_ref,
    got_gain_ref, own_weight_ref, got_weight_ref, own_ref, other_ref, *rest,
):
    *out_refs, term_ref = rest
    mixed = own_part_ref[...]
    for ref in (one_ref, two_ref, three_ref):
        mixed = mixed + ref[...].astype(F32)
    half = mixed.shape[1] // 2
    first = place_ref[1] == 0
    left, right = mixed[:, :half], mixed[:, half:]
    rows = mixed.shape[0]
    residual = residual_ref[pl.ds(pl.multiple_of(place_ref[1] * rows, rows), rows), :].astype(F32)
    term, squares = 0.0, 0.0
    for piece, gain_ref, weight_ref, layer_ref in (
        (jnp.where(first, left, right) + residual, own_gain_ref, own_weight_ref, own_ref),
        (jnp.where(first, right, left), got_gain_ref, got_weight_ref, other_ref),
    ):
        layer = piece.astype(BF)
        layer_ref[...] = layer
        stream = layer.astype(F32)
        square = stream * stream
        upper = square.astype(BF)
        for value in (upper, (square - upper.astype(F32)).astype(BF)):
            squares = squares + lax.dot_general(
                jnp.ones((16, half), BF), value, (((1,), (1,)), ((), ())),
                preferred_element_type=F32,
            )
        term = term + jnp.dot(
            (stream * gain_ref[...]).astype(BF), weight_ref[...], preferred_element_type=F32
        )
    term_ref[...] = term.astype(BF)
    squares = squares.astype(BF)
    first_axis = jnp.where(first, place_ref[3], place_ref[4])
    for shift, ref in enumerate(out_refs):
        far = lax.rem(first_axis + shift, SIDE)
        for second in range(SIDE):
            j = jnp.where(first, far * SIDE + second, second * SIDE + far)
            ref[second, :BLK, :] = term_ref[:, pl.ds(pl.multiple_of(j * HEAD, HEAD), HEAD)]
            ref[second, BLK:, :] = squares


def tile_kernel(
    place_ref, own_part_ref, one_ref, two_ref, three_ref, own_layer_ref, got_layer_ref,
    tile_ref, layer_ref,
):
    for ref, half in ((own_layer_ref, place_ref[1]), (got_layer_ref, 1 - place_ref[1])):
        rows = ref.shape[0]
        layer_ref[pl.ds(pl.multiple_of(half * rows, rows), rows), :] = ref[...]
    total = own_part_ref[...].astype(F32)
    for ref in (one_ref, two_ref, three_ref):
        total = total + ref[...].astype(F32)
    scale = lax.rsqrt(total[0, BLK : BLK + 1, :] / D + EPS)
    column = jnp.transpose(jnp.broadcast_to(scale, (BLK, BLK)))
    tile_ref[...] = (total[:, :BLK, :] * column[None]).astype(BF)


def choose(place_ref, target, starts_ref, counts_ref, sources, out_ref):
    first, count = starts_ref[target], counts_ref[target]
    slot = lax.rem(place_ref[1] + first, 2)
    for i, ref in enumerate(sources):
        for second in range(SIDE):
            for k in range(2):
                at = slot + 2 * k
                tile = ref[jnp.minimum((first + at) // 2, SIDE - 1), second]
                out_ref[k, i * SIDE + second] = jnp.where(at < count, tile, jnp.zeros_like(tile))


def to_cache(place_ref, starts_ref, core, source_refs, cache_ref, sems):
    slot = lax.rem(core + starts_ref[place_ref[2]], 2)
    waits = []
    for i, shift in enumerate((0, EARLY, *LATE)):
        source_ref = source_refs[i // (SIDE // len(source_refs))]
        first_axis = lax.rem(jnp.where(core == 0, place_ref[3], place_ref[4]) + SIDE - shift, SIDE)
        at = i * SIDE % source_ref.shape[1]
        for k in range(2):
            part = source_ref.at[k, pl.ds(at, SIDE)]
            along_y = pltpu.make_async_copy(
                part, cache_ref.at[slot + 2 * k, first_axis], sems.at[k, i]
            )
            along_x = pltpu.make_async_copy(
                part, cache_ref.at[slot + 2 * k, :, first_axis], sems.at[k, i]
            )
            pl.when(core == 0)(along_y.start)
            pl.when(core == 1)(along_x.start)
            waits.append(along_y)
    for copy in waits:
        copy.wait()


def stack_kernel(place_ref, own_ref, near_ref, mid_ref, far_ref, out_ref):
    for back, ref in enumerate((own_ref, near_ref, mid_ref, far_ref)):
        out_ref[lax.rem(place_ref[0] + SIDE - back, SIDE)] = ref[...]


def pick_kernel(place_ref, starts_ref, counts_ref, one_ref, two_ref, out_ref):
    partner = place_ref[2] + 1 - 2 * place_ref[1]
    choose(place_ref, partner, starts_ref, counts_ref, (one_ref, two_ref), out_ref)


def own_kernel(place_ref, starts_ref, counts_ref, q0, q1, q2, q3, cache_ref, held_ref, sems):
    choose(place_ref, place_ref[2], starts_ref, counts_ref, (q0, q1, q2, q3), held_ref)
    to_cache(place_ref, starts_ref, place_ref[1], (held_ref,), cache_ref, sems)


def rest_kernel(place_ref, starts_ref, one_ref, two_ref, _, cache_ref, sems):
    to_cache(place_ref, starts_ref, 1 - place_ref[1], (one_ref, two_ref), cache_ref, sems)


def shape(dims, kind):
    return jax.ShapeDtypeStruct(dims, kind)


def per_device(
    conv_out,
    gate_in,
    residual,
    xproj_weight,
    dtproj_weight,
    dt_bias,
    a_log,
    d_skip,
    init_state,
    out_weight,
    norm_gain,
    kv_weight,
    owner,
    block_start,
    block_count,
):
    tp_count = lax.axis_size("tp")
    ctx_count = lax.axis_size("ctx")
    tokens, chans = conv_out.shape
    feats = residual.shape[1]
    pairs = tp_count // 2
    place = lax.axis_index("ctx")
    member = lax.axis_index("tp")
    core = member % 2
    places = jnp.stack(
        [
            place, core, place * tp_count + member,
            member // (2 * SIDE), (member // 2) % SIDE,
        ]
    ).astype(jnp.int32)
    partner = [(i, i ^ 1) for i in range(tp_count)]

    def line(stage, value_of):
        return [
            lax.ppermute(
                value_of(shift),
                "tp",
                [
                    (
                        (x * SIDE + y) * 2 + c,
                        ((x + shift) % SIDE * SIDE + y) * 2 + c
                        if c == stage
                        else (x * SIDE + (y + shift) % SIDE) * 2 + c,
                    )
                    for x in range(SIDE)
                    for y in range(SIDE)
                    for c in range(2)
                ],
            )
            for shift in range(1, SIDE)
        ]

    def swap(value):
        return lax.ppermute(value, "tp", partner)

    own_gain = norm_gain.reshape(1, feats)
    got_gain, got_weight = swap(own_gain), swap(kv_weight)
    devices = owner.shape[0]
    matches = owner[:, None] == jnp.arange(devices, dtype=jnp.int32)[None, :]
    starts = jnp.sum(jnp.where(matches, block_start[:, None], 0), axis=0)
    counts = jnp.sum(jnp.where(matches, block_count[:, None], 0), axis=0)

    def add(name, kind, *values):
        return pl.pallas_call(
            add_kernel,
            out_shape=shape(values[0].shape, kind),
            compiler_params=params(8),
            name=name,
        )(*values)

    def project(name, give, kind):
        return pl.pallas_call(
            functools.partial(project_kernel, give),
            in_specs=[SM] + [VM] * 2,
            out_shape=shape((BLK + 16, DTR), kind),
            compiler_params=params(8),
            name=name,
        )(places, conv_out, xproj_weight.T)

    give_share = project("project_give", True, BF)
    kept_share = project("project_keep", False, F32)
    got_share, got_gain = lax.optimization_barrier((swap(give_share), got_gain))
    chip = add("chip", BF, kept_share, got_share)
    row = add("row", BF, chip, *line(0, lambda shift: chip))
    own_proj = add("plane", BF, row, *line(1, lambda shift: row))

    blocks = tokens // CHUNK
    step, states, ends = pl.pallas_call(
        first_kernel,
        out_shape=(
            shape((tokens, chans), F32),
            shape((blocks, 2 * STATE, CHUNK), F32),
            shape((STATE + 8, chans), F32),
        ),
        in_specs=[SM] + [VM] * 6,
        scratch_shapes=[
            pltpu.VMEM((tokens, DTR), BF),
            pltpu.VMEM((tokens, chans), F32),
        ],
        compiler_params=params(8),
        name="first",
    )(places, own_proj, swap(own_proj), dtproj_weight, dt_bias.reshape(1, chans), a_log, conv_out)
    def ranges_back(value):
        return [
            lax.ppermute(value, "ctx", [(z, (z + s) % ctx_count) for z in range(ctx_count)])
            for s in range(1, ctx_count)
        ]

    near_weight = pl.pallas_call(
        bring_kernel,
        in_specs=[ANY] * 2,
        out_shape=shape(out_weight.shape, BF),
        scratch_shapes=[pltpu.SemaphoreType.DMA((PIECES,))],
        compiler_params=params(42),
        name="bring",
    )(out_weight, ends)
    partial = (pairs, tokens // 2, 2 * feats)
    give, kept = pl.pallas_call(
        give_kernel,
        in_specs=[SM] + [VM] * 12,
        out_shape=(shape(partial, BF), shape((tokens // 2, chans), BF)),
        scratch_shapes=[
            pltpu.VMEM((tokens, chans), F32),
            pltpu.VMEM((tokens, chans), F32),
            pltpu.VMEM((2, tokens // 2, chans), BF),
        ],
        compiler_params=params(20),
        name="give",
    )(
        places, step, states, a_log, conv_out, gate_in, d_skip.reshape(1, chans), init_state,
        *ranges_back(ends), near_weight, residual,
    )
    got = swap(give)
    keep = pl.pallas_call(
        keep_kernel,
        in_specs=[SM, VM, VM],
        out_shape=shape(partial, BF),
        compiler_params=params(16),
        name="keep",
    )(places, kept, near_weight)
    quarter = shape((SIDE, tokens // 2, 2 * feats), BF)
    sums = pl.pallas_call(
        pair_kernel, out_shape=(quarter,) * SIDE, compiler_params=params(12), name="pair"
    )(keep, got)
    row = (tokens // 2, 2 * feats)
    parts = pl.pallas_call(
        line_kernel,
        out_shape=(shape(row, F32),) + (shape(row, BF),) * (SIDE - 1),
        compiler_params=params(12),
        name="line",
    )(sums[0], *line(0, lambda shift: sums[shift]))
    parts = [parts[0]] + line(1, lambda shift: parts[shift])

    block_shape = shape((tokens // 2, feats), BF)
    own_layer, other_layer, *kv_terms = pl.pallas_call(
        layer_kernel,
        in_specs=[SM] + [VM] * 9,
        out_shape=(block_shape,) * 2 + (shape((SIDE, BLK + 16, HEAD), BF),) * SIDE,
        scratch_shapes=[pltpu.VMEM((tokens // 2, 2 * KVH * HEAD), BF)],
        compiler_params=params(8),
        name="layer",
    )(places, *parts, residual, own_gain, got_gain, kv_weight, got_weight)
    got_layer = swap(other_layer)
    kv_row = add("kv", BF, kv_terms[0], *line(0, lambda shift: kv_terms[shift]))
    tile, layer_out = pl.pallas_call(
        tile_kernel,
        in_specs=[SM] + [VM] * 6,
        out_shape=(shape((SIDE, BLK, HEAD), BF), shape((tokens, feats), BF)),
        compiler_params=params(8),
        name="tile",
    )(places, kv_row, *line(1, lambda shift: kv_row), own_layer, got_layer)
    stacked = pl.pallas_call(
        stack_kernel,
        in_specs=[SM] + [VM] * 4,
        out_shape=shape((ctx_count, SIDE, BLK, HEAD), BF),
        compiler_params=params(4),
        name="stack",
    )(places, tile, *ranges_back(tile))
    everything = [stacked] + line(0, lambda shift: stacked)
    chosen = (2, 2 * SIDE, BLK, HEAD)
    sems = pltpu.SemaphoreType.DMA((2, SIDE))
    cache_shape = shape((CAP, SIDE, SIDE, BLK, HEAD), BF)

    def for_partner(name, *sources):
        return swap(
            pl.pallas_call(
                pick_kernel,
                in_specs=[SM] * 3 + [VM] * 2,
                out_shape=shape(chosen, BF),
                compiler_params=params(4),
                name=name,
            )(places, starts, counts, *sources)
        )

    got_first = for_partner("pick0", everything[0], everything[EARLY])
    *late, got_first = lax.optimization_barrier((*[everything[i] for i in LATE], got_first))
    everything = [everything[0], everything[EARLY], *late]
    got_last = for_partner("pick1", *late)
    kv_cache = pl.pallas_call(
        own_kernel,
        in_specs=[SM] * 3 + [VM] * SIDE,
        out_specs=ANY,
        out_shape=cache_shape,
        scratch_shapes=[pltpu.VMEM((2, 4 * SIDE, BLK, HEAD), BF), sems],
        compiler_params=params(8),
        name="own",
    )(places, starts, counts, *everything)
    kv_cache = pl.pallas_call(
        rest_kernel,
        in_specs=[SM] * 2 + [VM, VM, ANY],
        out_specs=ANY,
        out_shape=cache_shape,
        input_output_aliases={4: 0},
        scratch_shapes=[sems],
        compiler_params=params(4),
        name="rest",
    )(places, starts, got_first, got_last, kv_cache)
    return (layer_out, kv_cache.reshape(1, CAP, 2 * KVH, BLK, HEAD))


def solution(mesh):
    placed = (
        P("ctx", "tp"),
        P("ctx", "tp"),
        P("ctx", "tp"),
        P("tp", None),
        P(None, "tp"),
        P("tp"),
        P(None, "tp"),
        P("tp"),
        P(None, "tp"),
        P("tp", None),
        P("tp"),
        P("tp", None),
        P(),
        P(),
        P(),
    )
    return jax.shard_map(
        per_device,
        mesh=mesh,
        in_specs=placed,
        out_specs=(P("ctx", "tp"), P(("ctx", "tp"), None, None, None, None)),
        check_vma=False,
    )
```

```python
import functools

import jax
import jax.numpy as jnp
from jax import lax
from jax.experimental import pallas as pl
from jax.experimental.pallas import tpu as pltpu
from jax.sharding import PartitionSpec as P

D = 8192
STATE = 16
DTR = 512
KVH = 8
HEAD = 128
BLK = 128
CAP = 4
EPS = 1e-05
LOG2E = 1.4426950408889634
CHUNK = 64
PIECES = 8
SIDE = 4
SOON, LATER = (1, 2), (0, 3)
EARLY, LATE = 1, (2, 3)
BF = jnp.bfloat16
F32 = jnp.float32

VM = pl.BlockSpec(memory_space=pltpu.VMEM)
SM = pl.BlockSpec(memory_space=pltpu.SMEM)
ANY = pl.BlockSpec(memory_space=pl.ANY)


def params(mib):
    return pltpu.CompilerParams(vmem_limit_bytes=mib * 1024 * 1024)


def project_kernel(give, place_ref, conv_ref, weight_ref, out_ref):
    half = 1 - place_ref[1] if give else place_ref[1]
    conv = conv_ref[pl.ds(pl.multiple_of(half * BLK, BLK), BLK), :]
    both = (((1,), (1,)), ((), ()))
    out_ref[:BLK, :] = lax.dot_general(
        conv, weight_ref[:DTR, :], both, preferred_element_type=F32
    ).astype(out_ref.dtype)
    states = lax.dot_general(weight_ref[DTR:, :], conv, both, preferred_element_type=F32)
    packed = [states[i * 8 : (i + 1) * 8, :] for i in range(DTR // BLK)]
    packed = jnp.concatenate(packed, axis=1)
    out_ref[BLK:, :] = jnp.concatenate([packed, jnp.zeros_like(packed)], axis=0).astype(out_ref.dtype)


def add_kernel(*refs):
    total = refs[0][...].astype(F32)
    for ref in refs[1:-1]:
        total = total + ref[...].astype(F32)
    refs[-1][...] = total.astype(refs[-1].dtype)


def fold_rows(values):
    row = lax.broadcasted_iota(jnp.int32, values[0].shape, 0)
    for reach in (4, 2, 1):
        near = row % (2 * reach) < reach
        values = [
            jnp.where(near, a, b)
            + jnp.where(near, pltpu.roll(a, 8 - reach, 0), pltpu.roll(b, reach, 0))
            for a, b in zip(values[:reach], values[reach:], strict=True)
        ]
    return values[0]


def advance_block(block, hidden, step_ref, drive_ref, states_ref, rates, read_out):
    states = states_ref[block]
    for group in range(CHUNK // 8):
        rows = pl.ds(pl.multiple_of(block * CHUNK + group * 8, 8), 8)
        steps, drives = step_ref[rows, :], drive_ref[rows, :]
        outs = []
        for i in range(8):
            at = group * 8 + i
            decay = jnp.exp2(steps[i : i + 1, :] * rates)
            hidden = decay * hidden + states[:STATE, at : at + 1] * drives[i : i + 1, :]
            if read_out is not None:
                terms = hidden * states[STATE:, at : at + 1]
                outs.append(terms[:8] + terms[8:])
        if read_out is not None:
            read_out[rows, :] = fold_rows(outs)
    return hidden


def first_kernel(
    place_ref, own_proj_ref, got_proj_ref, weight_ref, bias_ref, alog_ref, conv_ref,
    step_ref, states_ref, ends_ref, proj_ref, drive_ref,
):
    tokens = step_ref.shape[0]
    for ref, half in ((own_proj_ref, place_ref[1]), (got_proj_ref, 1 - place_ref[1])):
        proj_ref[pl.ds(pl.multiple_of(half * BLK, BLK), BLK), :] = ref[:BLK, :]
        packed = ref[BLK:, :].astype(F32)
        for group in range(DTR // BLK):
            for block in range(BLK // CHUNK):
                at = group * BLK + block * CHUNK
                states_ref[half * (BLK // CHUNK) + block, group * 8 : (group + 1) * 8, :] = (
                    packed[:8, at : at + CHUNK]
                )
    step = jax.nn.softplus(
        jnp.dot(proj_ref[...], weight_ref[...], preferred_element_type=F32) + bias_ref[...]
    )
    step_ref[...] = step
    drive_ref[...] = step * conv_ref[...].astype(F32)
    rates = -jnp.exp(alog_ref[...]) * LOG2E
    hidden = lax.fori_loop(
        0,
        tokens // CHUNK,
        lambda k, h: advance_block(k, h, step_ref, drive_ref, states_ref, rates, None),
        jnp.zeros_like(rates),
    )
    ends_ref[:STATE, :] = hidden
    ends_ref[STATE:, :] = jnp.broadcast_to(jnp.sum(step, axis=0, keepdims=True), (8, step.shape[1]))


def give_kernel(
    place_ref, step_ref, states_ref, alog_ref, conv_ref, gate_ref, skip_ref, init_ref,
    near_ref, mid_ref, far_ref, weight_ref, residual_ref,
    soon_ref, give_ref, kept_ref, drive_ref, scan_ref, gated_ref,
):
    tokens = step_ref.shape[0]
    place, core = place_ref[0], place_ref[1]
    rates = -jnp.exp(alog_ref[...]) * LOG2E
    hidden = init_ref[...]
    for back, ref in ((3, far_ref), (2, mid_ref), (1, near_ref)):
        passed = jnp.exp2(ref[STATE : STATE + 1, :] * rates) * hidden + ref[:STATE, :]
        hidden = jnp.where(place >= back, passed, hidden)
    drive_ref[...] = step_ref[...] * conv_ref[...].astype(F32)
    lax.fori_loop(
        0,
        tokens // CHUNK,
        lambda k, h: advance_block(k, h, step_ref, drive_ref, states_ref, rates, scan_ref),
        hidden,
    )
    gate = gate_ref[...].astype(F32)
    gated_ref[...] = (
        (scan_ref[...] + skip_ref[...] * conv_ref[...].astype(F32)) * (gate / (1.0 + jnp.exp(-gate)))
    ).astype(BF).reshape(gated_ref.shape)
    kept_ref[...] = gated_ref[core]
    through(place_ref, 1 - core, gated_ref.at[1 - core], weight_ref, ((SOON, soon_ref), (LATER, give_ref)))
    rows, feats = residual_ref.shape[0] // 2, residual_ref.shape[1]
    mine = pl.ds(pl.multiple_of(core * feats, feats), feats)
    other = residual_ref[pl.ds(pl.multiple_of((1 - core) * rows, rows), rows), :]
    give_ref[0, :, mine] = (give_ref[0, :, mine].astype(F32) + other.astype(F32)).astype(BF)


def bring_kernel(weight_ref, _, held_ref, sems):
    wide = weight_ref.shape[1] // PIECES
    copies = [
        pltpu.make_async_copy(
            weight_ref.at[:, pl.ds(i * wide, wide)], held_ref.at[:, pl.ds(i * wide, wide)],
            sems.at[i],
        )
        for i in range(PIECES)
    ]
    for copy in copies:
        copy.start()
    for copy in copies:
        copy.wait()


def through(place_ref, core, gated_ref, weight_ref, parts):
    for fars, out_ref in parts:
        wide = out_ref.shape[2]
        for i, far in enumerate(fars):
            for near in range(SIDE):
                x = lax.rem(place_ref[3] + jnp.where(core == 0, far, near), SIDE)
                y = lax.rem(place_ref[4] + jnp.where(core == 0, near, far), SIDE)
                columns = pl.ds(pl.multiple_of((x * SIDE + y) * wide, wide), wide)
                out_ref[i * SIDE + near] = jnp.dot(
                    gated_ref[...], weight_ref[:, columns], preferred_element_type=F32
                ).astype(BF)


def keep_kernel(place_ref, kept_ref, weight_ref, keep_ref):
    through(place_ref, place_ref[1], kept_ref, weight_ref, ((range(SIDE), keep_ref),))


def pair_kernel(fars, keep_ref, got_ref, *out_refs):
    for i, (far, ref) in enumerate(zip(fars, out_refs, strict=True)):
        kept = keep_ref[far * SIDE : (far + 1) * SIDE]
        got = got_ref[i * SIDE : (i + 1) * SIDE]
        ref[...] = (kept.astype(F32) + got.astype(F32)).astype(ref.dtype)


def line_kernel(own_ref, one_ref, two_ref, three_ref, *out_refs):
    for shift, ref in enumerate(out_refs):
        total = own_ref[shift].astype(F32)
        for other in (one_ref, two_ref, three_ref):
            total = total + other[shift].astype(F32)
        ref[...] = total.astype(ref.dtype)


def layer_kernel(
    place_ref, own_part_ref, one_ref, two_ref, three_ref, residual_ref, own_gain_ref,
    got_gain_ref, own_weight_ref, got_weight_ref, own_ref, other_ref, *rest,
):
    *out_refs, term_ref = rest
    mixed = own_part_ref[...]
    for ref in (one_ref, two_ref, three_ref):
        mixed = mixed + ref[...].astype(F32)
    half = mixed.shape[1] // 2
    first = place_ref[1] == 0
    left, right = mixed[:, :half], mixed[:, half:]
    rows = mixed.shape[0]
    residual = residual_ref[pl.ds(pl.multiple_of(place_ref[1] * rows, rows), rows), :].astype(F32)
    term, squares = 0.0, 0.0
    for piece, gain_ref, weight_ref, layer_ref in (
        (jnp.where(first, left, right) + residual, own_gain_ref, own_weight_ref, own_ref),
        (jnp.where(first, right, left), got_gain_ref, got_weight_ref, other_ref),
    ):
        layer = piece.astype(BF)
        layer_ref[...] = layer
        stream = layer.astype(F32)
        square = stream * stream
        upper = square.astype(BF)
        for value in (upper, (square - upper.astype(F32)).astype(BF)):
            squares = squares + lax.dot_general(
                jnp.ones((16, half), BF), value, (((1,), (1,)), ((), ())),
                preferred_element_type=F32,
            )
        term = term + jnp.dot(
            (stream * gain_ref[...]).astype(BF), weight_ref[...], preferred_element_type=F32
        )
    term_ref[...] = term.astype(BF)
    squares = squares.astype(BF)
    first_axis = jnp.where(first, place_ref[3], place_ref[4])
    for shift, ref in enumerate(out_refs):
        far = lax.rem(first_axis + shift, SIDE)
        for second in range(SIDE):
            j = jnp.where(first, far * SIDE + second, second * SIDE + far)
            ref[second, :BLK, :] = term_ref[:, pl.ds(pl.multiple_of(j * HEAD, HEAD), HEAD)]
            ref[second, BLK:, :] = squares


def tile_kernel(
    place_ref, own_part_ref, one_ref, two_ref, three_ref, own_layer_ref, got_layer_ref,
    tile_ref, layer_ref,
):
    for ref, half in ((own_layer_ref, place_ref[1]), (got_layer_ref, 1 - place_ref[1])):
        rows = ref.shape[0]
        layer_ref[pl.ds(pl.multiple_of(half * rows, rows), rows), :] = ref[...]
    total = own_part_ref[...].astype(F32)
    for ref in (one_ref, two_ref, three_ref):
        total = total + ref[...].astype(F32)
    scale = lax.rsqrt(total[0, BLK : BLK + 1, :] / D + EPS)
    column = jnp.transpose(jnp.broadcast_to(scale, (BLK, BLK)))
    tile_ref[...] = (total[:, :BLK, :] * column[None]).astype(BF)


def choose(place_ref, target, starts_ref, counts_ref, sources, out_ref):
    first, count = starts_ref[target], counts_ref[target]
    slot = lax.rem(place_ref[1] + first, 2)
    for i, ref in enumerate(sources):
        for second in range(SIDE):
            for k in range(2):
                at = slot + 2 * k
                tile = ref[jnp.minimum((first + at) // 2, SIDE - 1), second]
                out_ref[k, i * SIDE + second] = jnp.where(at < count, tile, jnp.zeros_like(tile))


def to_cache(place_ref, starts_ref, core, source_refs, cache_ref, sems):
    slot = lax.rem(core + starts_ref[place_ref[2]], 2)
    waits = []
    for i, shift in enumerate((0, EARLY, *LATE)):
        source_ref = source_refs[i // (SIDE // len(source_refs))]
        first_axis = lax.rem(jnp.where(core == 0, place_ref[3], place_ref[4]) + SIDE - shift, SIDE)
        at = i * SIDE % source_ref.shape[1]
        for k in range(2):
            part = source_ref.at[k, pl.ds(at, SIDE)]
            along_y = pltpu.make_async_copy(
                part, cache_ref.at[slot + 2 * k, first_axis], sems.at[k, i]
            )
            along_x = pltpu.make_async_copy(
                part, cache_ref.at[slot + 2 * k, :, first_axis], sems.at[k, i]
            )
            pl.when(core == 0)(along_y.start)
            pl.when(core == 1)(along_x.start)
            waits.append(along_y)
    for copy in waits:
        copy.wait()


def stack_kernel(place_ref, own_ref, near_ref, mid_ref, far_ref, out_ref):
    for back, ref in enumerate((own_ref, near_ref, mid_ref, far_ref)):
        out_ref[lax.rem(place_ref[0] + SIDE - back, SIDE)] = ref[...]


def pick_kernel(place_ref, starts_ref, counts_ref, one_ref, two_ref, out_ref):
    partner = place_ref[2] + 1 - 2 * place_ref[1]
    choose(place_ref, partner, starts_ref, counts_ref, (one_ref, two_ref), out_ref)


def own_kernel(place_ref, starts_ref, counts_ref, q0, q1, q2, q3, cache_ref, held_ref, sems):
    choose(place_ref, place_ref[2], starts_ref, counts_ref, (q0, q1, q2, q3), held_ref)
    to_cache(place_ref, starts_ref, place_ref[1], (held_ref,), cache_ref, sems)


def rest_kernel(place_ref, starts_ref, one_ref, two_ref, _, cache_ref, sems):
    to_cache(place_ref, starts_ref, 1 - place_ref[1], (one_ref, two_ref), cache_ref, sems)


def shape(dims, kind):
    return jax.ShapeDtypeStruct(dims, kind)


def per_device(
    conv_out,
    gate_in,
    residual,
    xproj_weight,
    dtproj_weight,
    dt_bias,
    a_log,
    d_skip,
    init_state,
    out_weight,
    norm_gain,
    kv_weight,
    owner,
    block_start,
    block_count,
):
    tp_count = lax.axis_size("tp")
    ctx_count = lax.axis_size("ctx")
    tokens, chans = conv_out.shape
    feats = residual.shape[1]
    pairs = tp_count // 2
    place = lax.axis_index("ctx")
    member = lax.axis_index("tp")
    core = member % 2
    places = jnp.stack(
        [
            place, core, place * tp_count + member,
            member // (2 * SIDE), (member // 2) % SIDE,
        ]
    ).astype(jnp.int32)
    partner = [(i, i ^ 1) for i in range(tp_count)]

    def line(stage, value_of):
        return [
            lax.ppermute(
                value_of(shift),
                "tp",
                [
                    (
                        (x * SIDE + y) * 2 + c,
                        ((x + shift) % SIDE * SIDE + y) * 2 + c
                        if c == stage
                        else (x * SIDE + (y + shift) % SIDE) * 2 + c,
                    )
                    for x in range(SIDE)
                    for y in range(SIDE)
                    for c in range(2)
                ],
            )
            for shift in range(1, SIDE)
        ]

    def swap(value):
        return lax.ppermute(value, "tp", partner)

    own_gain = norm_gain.reshape(1, feats)
    got_gain, got_weight = swap(own_gain), swap(kv_weight)
    devices = owner.shape[0]
    matches = owner[:, None] == jnp.arange(devices, dtype=jnp.int32)[None, :]
    starts = jnp.sum(jnp.where(matches, block_start[:, None], 0), axis=0)
    counts = jnp.sum(jnp.where(matches, block_count[:, None], 0), axis=0)

    def add(name, kind, *values):
        return pl.pallas_call(
            add_kernel,
            out_shape=shape(values[0].shape, kind),
            compiler_params=params(8),
            name=name,
        )(*values)

    def project(name, give, kind):
        return pl.pallas_call(
            functools.partial(project_kernel, give),
            in_specs=[SM] + [VM] * 2,
            out_shape=shape((BLK + 16, DTR), kind),
            compiler_params=params(8),
            name=name,
        )(places, conv_out, xproj_weight.T)

    give_share = project("project_give", True, BF)
    kept_share = project("project_keep", False, F32)
    got_share, got_gain = lax.optimization_barrier((swap(give_share), got_gain))
    chip = add("chip", BF, kept_share, got_share)
    row = add("row", BF, chip, *line(0, lambda shift: chip))
    own_proj = add("plane", BF, row, *line(1, lambda shift: row))

    blocks = tokens // CHUNK
    step, states, ends = pl.pallas_call(
        first_kernel,
        out_shape=(
            shape((tokens, chans), F32),
            shape((blocks, 2 * STATE, CHUNK), F32),
            shape((STATE + 8, chans), F32),
        ),
        in_specs=[SM] + [VM] * 6,
        scratch_shapes=[
            pltpu.VMEM((tokens, DTR), BF),
            pltpu.VMEM((tokens, chans), F32),
        ],
        compiler_params=params(8),
        name="first",
    )(places, own_proj, swap(own_proj), dtproj_weight, dt_bias.reshape(1, chans), a_log, conv_out)
    def ranges_back(value):
        return [
            lax.ppermute(value, "ctx", [(z, (z + s) % ctx_count) for z in range(ctx_count)])
            for s in range(1, ctx_count)
        ]

    near_weight = pl.pallas_call(
        bring_kernel,
        in_specs=[ANY] * 2,
        out_shape=shape(out_weight.shape, BF),
        scratch_shapes=[pltpu.SemaphoreType.DMA((PIECES,))],
        compiler_params=params(42),
        name="bring",
    )(out_weight, ends)
    partial = (pairs, tokens // 2, 2 * feats)
    half = (pairs // 2,) + partial[1:]
    soon, give, kept = pl.pallas_call(
        give_kernel,
        in_specs=[SM] + [VM] * 12,
        out_shape=(shape(half, BF), shape(half, BF), shape((tokens // 2, chans), BF)),
        scratch_shapes=[
            pltpu.VMEM((tokens, chans), F32),
            pltpu.VMEM((tokens, chans), F32),
            pltpu.VMEM((2, tokens // 2, chans), BF),
        ],
        compiler_params=params(20),
        name="give",
    )(
        places, step, states, a_log, conv_out, gate_in, d_skip.reshape(1, chans), init_state,
        *ranges_back(ends), near_weight, residual,
    )
    got_soon, got = swap(soon), swap(give)
    keep = pl.pallas_call(
        keep_kernel,
        in_specs=[SM, VM, VM],
        out_shape=shape(partial, BF),
        compiler_params=params(16),
        name="keep",
    )(places, kept, near_weight)
    quarter = shape((SIDE, tokens // 2, 2 * feats), BF)
    def pair(name, fars, got):
        return pl.pallas_call(
            functools.partial(pair_kernel, fars),
            out_shape=(quarter,) * 2,
            compiler_params=params(12),
            name=name,
        )(keep, got)

    sums = dict(zip(SOON, pair("pair_soon", SOON, got_soon), strict=True))
    sums.update(zip(LATER, pair("pair", LATER, got), strict=True))
    row = (tokens // 2, 2 * feats)
    parts = pl.pallas_call(
        line_kernel,
        out_shape=(shape(row, F32),) + (shape(row, BF),) * (SIDE - 1),
        compiler_params=params(12),
        name="line",
    )(sums[0], *line(0, lambda shift: sums[shift]))
    parts = [parts[0]] + line(1, lambda shift: parts[shift])

    block_shape = shape((tokens // 2, feats), BF)
    own_layer, other_layer, *kv_terms = pl.pallas_call(
        layer_kernel,
        in_specs=[SM] + [VM] * 9,
        out_shape=(block_shape,) * 2 + (shape((SIDE, BLK + 16, HEAD), BF),) * SIDE,
        scratch_shapes=[pltpu.VMEM((tokens // 2, 2 * KVH * HEAD), BF)],
        compiler_params=params(8),
        name="layer",
    )(places, *parts, residual, own_gain, got_gain, kv_weight, got_weight)
    got_layer = swap(other_layer)
    kv_row = add("kv", BF, kv_terms[0], *line(0, lambda shift: kv_terms[shift]))
    tile, layer_out = pl.pallas_call(
        tile_kernel,
        in_specs=[SM] + [VM] * 6,
        out_shape=(shape((SIDE, BLK, HEAD), BF), shape((tokens, feats), BF)),
        compiler_params=params(8),
        name="tile",
    )(places, kv_row, *line(1, lambda shift: kv_row), own_layer, got_layer)
    stacked = pl.pallas_call(
        stack_kernel,
        in_specs=[SM] + [VM] * 4,
        out_shape=shape((ctx_count, SIDE, BLK, HEAD), BF),
        compiler_params=params(4),
        name="stack",
    )(places, tile, *ranges_back(tile))
    everything = [stacked] + line(0, lambda shift: stacked)
    chosen = (2, 2 * SIDE, BLK, HEAD)
    sems = pltpu.SemaphoreType.DMA((2, SIDE))
    cache_shape = shape((CAP, SIDE, SIDE, BLK, HEAD), BF)

    def for_partner(name, *sources):
        return swap(
            pl.pallas_call(
                pick_kernel,
                in_specs=[SM] * 3 + [VM] * 2,
                out_shape=shape(chosen, BF),
                compiler_params=params(4),
                name=name,
            )(places, starts, counts, *sources)
        )

    got_first = for_partner("pick0", everything[0], everything[EARLY])
    *late, got_first = lax.optimization_barrier((*[everything[i] for i in LATE], got_first))
    everything = [everything[0], everything[EARLY], *late]
    got_last = for_partner("pick1", *late)
    kv_cache = pl.pallas_call(
        own_kernel,
        in_specs=[SM] * 3 + [VM] * SIDE,
        out_specs=ANY,
        out_shape=cache_shape,
        scratch_shapes=[pltpu.VMEM((2, 4 * SIDE, BLK, HEAD), BF), sems],
        compiler_params=params(8),
        name="own",
    )(places, starts, counts, *everything)
    kv_cache = pl.pallas_call(
        rest_kernel,
        in_specs=[SM] * 2 + [VM, VM, ANY],
        out_specs=ANY,
        out_shape=cache_shape,
        input_output_aliases={4: 0},
        scratch_shapes=[sems],
        compiler_params=params(4),
        name="rest",
    )(places, starts, got_first, got_last, kv_cache)
    return (layer_out, kv_cache.reshape(1, CAP, 2 * KVH, BLK, HEAD))


def solution(mesh):
    placed = (
        P("ctx", "tp"),
        P("ctx", "tp"),
        P("ctx", "tp"),
        P("tp", None),
        P(None, "tp"),
        P("tp"),
        P(None, "tp"),
        P("tp"),
        P(None, "tp"),
        P("tp", None),
        P("tp"),
        P("tp", None),
        P(),
        P(),
        P(),
    )
    return jax.shard_map(
        per_device,
        mesh=mesh,
        in_specs=placed,
        out_specs=(P("ctx", "tp"), P(("ctx", "tp"), None, None, None, None)),
        check_vma=False,
    )
```

```python
import functools

import jax
import jax.numpy as jnp
from jax import lax
from jax.experimental import pallas as pl
from jax.experimental.pallas import tpu as pltpu
from jax.sharding import PartitionSpec as P

D = 8192
STATE = 16
DTR = 512
KVH = 8
HEAD = 128
BLK = 128
CAP = 4
EPS = 1e-05
LOG2E = 1.4426950408889634
CHUNK = 64
PIECES = 8
SIDE = 4
SOON, LATER = (2, 3), (0, 1)
EARLY, LATE = 1, (2, 3)
BF = jnp.bfloat16
F32 = jnp.float32

VM = pl.BlockSpec(memory_space=pltpu.VMEM)
SM = pl.BlockSpec(memory_space=pltpu.SMEM)
ANY = pl.BlockSpec(memory_space=pl.ANY)


def params(mib):
    return pltpu.CompilerParams(vmem_limit_bytes=mib * 1024 * 1024)


def project_kernel(give, place_ref, conv_ref, weight_ref, out_ref):
    half = 1 - place_ref[1] if give else place_ref[1]
    conv = conv_ref[pl.ds(pl.multiple_of(half * BLK, BLK), BLK), :]
    both = (((1,), (1,)), ((), ()))
    out_ref[:BLK, :] = lax.dot_general(
        conv, weight_ref[:DTR, :], both, preferred_element_type=F32
    ).astype(out_ref.dtype)
    states = lax.dot_general(weight_ref[DTR:, :], conv, both, preferred_element_type=F32)
    packed = [states[i * 8 : (i + 1) * 8, :] for i in range(DTR // BLK)]
    packed = jnp.concatenate(packed, axis=1)
    out_ref[BLK:, :] = jnp.concatenate([packed, jnp.zeros_like(packed)], axis=0).astype(out_ref.dtype)


def add_kernel(*refs):
    total = refs[0][...].astype(F32)
    for ref in refs[1:-1]:
        total = total + ref[...].astype(F32)
    refs[-1][...] = total.astype(refs[-1].dtype)


def fold_rows(values):
    row = lax.broadcasted_iota(jnp.int32, values[0].shape, 0)
    for reach in (4, 2, 1):
        near = row % (2 * reach) < reach
        values = [
            jnp.where(near, a, b)
            + jnp.where(near, pltpu.roll(a, 8 - reach, 0), pltpu.roll(b, reach, 0))
            for a, b in zip(values[:reach], values[reach:], strict=True)
        ]
    return values[0]


def advance_block(block, hidden, step_ref, drive_ref, states_ref, rates, read_out):
    states = states_ref[block]
    for group in range(CHUNK // 8):
        rows = pl.ds(pl.multiple_of(block * CHUNK + group * 8, 8), 8)
        steps, drives = step_ref[rows, :], drive_ref[rows, :]
        outs = []
        for i in range(8):
            at = group * 8 + i
            decay = jnp.exp2(steps[i : i + 1, :] * rates)
            hidden = decay * hidden + states[:STATE, at : at + 1] * drives[i : i + 1, :]
            if read_out is not None:
                terms = hidden * states[STATE:, at : at + 1]
                outs.append(terms[:8] + terms[8:])
        if read_out is not None:
            read_out[rows, :] = fold_rows(outs)
    return hidden


def first_kernel(
    place_ref, own_proj_ref, got_proj_ref, weight_ref, bias_ref, alog_ref, conv_ref,
    step_ref, states_ref, ends_ref, proj_ref, drive_ref,
):
    tokens = step_ref.shape[0]
    for ref, half in ((own_proj_ref, place_ref[1]), (got_proj_ref, 1 - place_ref[1])):
        proj_ref[pl.ds(pl.multiple_of(half * BLK, BLK), BLK), :] = ref[:BLK, :]
        packed = ref[BLK:, :].astype(F32)
        for group in range(DTR // BLK):
            for block in range(BLK // CHUNK):
                at = group * BLK + block * CHUNK
                states_ref[half * (BLK // CHUNK) + block, group * 8 : (group + 1) * 8, :] = (
                    packed[:8, at : at + CHUNK]
                )
    step = jax.nn.softplus(
        jnp.dot(proj_ref[...], weight_ref[...], preferred_element_type=F32) + bias_ref[...]
    )
    step_ref[...] = step
    drive_ref[...] = step * conv_ref[...].astype(F32)
    rates = -jnp.exp(alog_ref[...]) * LOG2E
    hidden = lax.fori_loop(
        0,
        tokens // CHUNK,
        lambda k, h: advance_block(k, h, step_ref, drive_ref, states_ref, rates, None),
        jnp.zeros_like(rates),
    )
    ends_ref[:STATE, :] = hidden
    ends_ref[STATE:, :] = jnp.broadcast_to(jnp.sum(step, axis=0, keepdims=True), (8, step.shape[1]))


def give_kernel(
    place_ref, step_ref, states_ref, alog_ref, conv_ref, gate_ref, skip_ref, init_ref,
    near_ref, mid_ref, far_ref, weight_ref, residual_ref,
    soon_ref, give_ref, kept_ref, drive_ref, scan_ref, gated_ref,
):
    tokens = step_ref.shape[0]
    place, core = place_ref[0], place_ref[1]
    rates = -jnp.exp(alog_ref[...]) * LOG2E
    hidden = init_ref[...]
    for back, ref in ((3, far_ref), (2, mid_ref), (1, near_ref)):
        passed = jnp.exp2(ref[STATE : STATE + 1, :] * rates) * hidden + ref[:STATE, :]
        hidden = jnp.where(place >= back, passed, hidden)
    drive_ref[...] = step_ref[...] * conv_ref[...].astype(F32)
    lax.fori_loop(
        0,
        tokens // CHUNK,
        lambda k, h: advance_block(k, h, step_ref, drive_ref, states_ref, rates, scan_ref),
        hidden,
    )
    gate = gate_ref[...].astype(F32)
    gated_ref[...] = (
        (scan_ref[...] + skip_ref[...] * conv_ref[...].astype(F32)) * (gate / (1.0 + jnp.exp(-gate)))
    ).astype(BF).reshape(gated_ref.shape)
    kept_ref[...] = gated_ref[core]
    through(place_ref, 1 - core, gated_ref.at[1 - core], weight_ref, ((SOON, soon_ref), (LATER, give_ref)))
    rows, feats = residual_ref.shape[0] // 2, residual_ref.shape[1]
    mine = pl.ds(pl.multiple_of(core * feats, feats), feats)
    other = residual_ref[pl.ds(pl.multiple_of((1 - core) * rows, rows), rows), :]
    give_ref[0, :, mine] = (give_ref[0, :, mine].astype(F32) + other.astype(F32)).astype(BF)


def bring_kernel(weight_ref, _, held_ref, sems):
    wide = weight_ref.shape[1] // PIECES
    copies = [
        pltpu.make_async_copy(
            weight_ref.at[:, pl.ds(i * wide, wide)], held_ref.at[:, pl.ds(i * wide, wide)],
            sems.at[i],
        )
        for i in range(PIECES)
    ]
    for copy in copies:
        copy.start()
    for copy in copies:
        copy.wait()


def through(place_ref, core, gated_ref, weight_ref, parts):
    for fars, out_ref in parts:
        wide = out_ref.shape[2]
        for i, far in enumerate(fars):
            for near in range(SIDE):
                x = lax.rem(place_ref[3] + jnp.where(core == 0, far, near), SIDE)
                y = lax.rem(place_ref[4] + jnp.where(core == 0, near, far), SIDE)
                columns = pl.ds(pl.multiple_of((x * SIDE + y) * wide, wide), wide)
                out_ref[i * SIDE + near] = jnp.dot(
                    gated_ref[...], weight_ref[:, columns], preferred_element_type=F32
                ).astype(BF)


def keep_kernel(place_ref, kept_ref, weight_ref, keep_ref):
    through(place_ref, place_ref[1], kept_ref, weight_ref, ((range(SIDE), keep_ref),))


def pair_kernel(fars, keep_ref, got_ref, *out_refs):
    for i, (far, ref) in enumerate(zip(fars, out_refs, strict=True)):
        kept = keep_ref[far * SIDE : (far + 1) * SIDE]
        got = got_ref[i * SIDE : (i + 1) * SIDE]
        ref[...] = (kept.astype(F32) + got.astype(F32)).astype(ref.dtype)


def line_kernel(own_ref, one_ref, two_ref, three_ref, *out_refs):
    for shift, ref in enumerate(out_refs):
        total = own_ref[shift].astype(F32)
        for other in (one_ref, two_ref, three_ref):
            total = total + other[shift].astype(F32)
        ref[...] = total.astype(ref.dtype)


def layer_kernel(
    place_ref, own_part_ref, one_ref, two_ref, three_ref, residual_ref, own_gain_ref,
    got_gain_ref, own_weight_ref, got_weight_ref, own_ref, other_ref, *rest,
):
    *out_refs, term_ref = rest
    mixed = own_part_ref[...]
    for ref in (one_ref, two_ref, three_ref):
        mixed = mixed + ref[...].astype(F32)
    half = mixed.shape[1] // 2
    first = place_ref[1] == 0
    left, right = mixed[:, :half], mixed[:, half:]
    rows = mixed.shape[0]
    residual = residual_ref[pl.ds(pl.multiple_of(place_ref[1] * rows, rows), rows), :].astype(F32)
    term, squares = 0.0, 0.0
    for piece, gain_ref, weight_ref, layer_ref in (
        (jnp.where(first, left, right) + residual, own_gain_ref, own_weight_ref, own_ref),
        (jnp.where(first, right, left), got_gain_ref, got_weight_ref, other_ref),
    ):
        layer = piece.astype(BF)
        layer_ref[...] = layer
        stream = layer.astype(F32)
        square = stream * stream
        upper = square.astype(BF)
        for value in (upper, (square - upper.astype(F32)).astype(BF)):
            squares = squares + lax.dot_general(
                jnp.ones((16, half), BF), value, (((1,), (1,)), ((), ())),
                preferred_element_type=F32,
            )
        term = term + jnp.dot(
            (stream * gain_ref[...]).astype(BF), weight_ref[...], preferred_element_type=F32
        )
    term_ref[...] = term.astype(BF)
    squares = squares.astype(BF)
    first_axis = jnp.where(first, place_ref[3], place_ref[4])
    for shift, ref in enumerate(out_refs):
        far = lax.rem(first_axis + shift, SIDE)
        for second in range(SIDE):
            j = jnp.where(first, far * SIDE + second, second * SIDE + far)
            ref[second, :BLK, :] = term_ref[:, pl.ds(pl.multiple_of(j * HEAD, HEAD), HEAD)]
            ref[second, BLK:, :] = squares


def tile_kernel(
    place_ref, own_part_ref, one_ref, two_ref, three_ref, own_layer_ref, got_layer_ref,
    tile_ref, layer_ref,
):
    for ref, half in ((own_layer_ref, place_ref[1]), (got_layer_ref, 1 - place_ref[1])):
        rows = ref.shape[0]
        layer_ref[pl.ds(pl.multiple_of(half * rows, rows), rows), :] = ref[...]
    total = own_part_ref[...].astype(F32)
    for ref in (one_ref, two_ref, three_ref):
        total = total + ref[...].astype(F32)
    scale = lax.rsqrt(total[0, BLK : BLK + 1, :] / D + EPS)
    column = jnp.transpose(jnp.broadcast_to(scale, (BLK, BLK)))
    tile_ref[...] = (total[:, :BLK, :] * column[None]).astype(BF)


def choose(place_ref, target, starts_ref, counts_ref, sources, out_ref):
    first, count = starts_ref[target], counts_ref[target]
    slot = lax.rem(place_ref[1] + first, 2)
    for i, ref in enumerate(sources):
        for second in range(SIDE):
            for k in range(2):
                at = slot + 2 * k
                tile = ref[jnp.minimum((first + at) // 2, SIDE - 1), second]
                out_ref[k, i * SIDE + second] = jnp.where(at < count, tile, jnp.zeros_like(tile))


def to_cache(place_ref, starts_ref, core, source_refs, cache_ref, sems):
    slot = lax.rem(core + starts_ref[place_ref[2]], 2)
    waits = []
    for i, shift in enumerate((0, EARLY, *LATE)):
        source_ref = source_refs[i // (SIDE // len(source_refs))]
        first_axis = lax.rem(jnp.where(core == 0, place_ref[3], place_ref[4]) + SIDE - shift, SIDE)
        at = i * SIDE % source_ref.shape[1]
        for k in range(2):
            part = source_ref.at[k, pl.ds(at, SIDE)]
            along_y = pltpu.make_async_copy(
                part, cache_ref.at[slot + 2 * k, first_axis], sems.at[k, i]
            )
            along_x = pltpu.make_async_copy(
                part, cache_ref.at[slot + 2 * k, :, first_axis], sems.at[k, i]
            )
            pl.when(core == 0)(along_y.start)
            pl.when(core == 1)(along_x.start)
            waits.append(along_y)
    for copy in waits:
        copy.wait()


def stack_kernel(place_ref, own_ref, near_ref, mid_ref, far_ref, out_ref):
    for back, ref in enumerate((own_ref, near_ref, mid_ref, far_ref)):
        out_ref[lax.rem(place_ref[0] + SIDE - back, SIDE)] = ref[...]


def pick_kernel(place_ref, starts_ref, counts_ref, one_ref, two_ref, out_ref):
    partner = place_ref[2] + 1 - 2 * place_ref[1]
    choose(place_ref, partner, starts_ref, counts_ref, (one_ref, two_ref), out_ref)


def own_kernel(place_ref, starts_ref, counts_ref, q0, q1, q2, q3, cache_ref, held_ref, sems):
    choose(place_ref, place_ref[2], starts_ref, counts_ref, (q0, q1, q2, q3), held_ref)
    to_cache(place_ref, starts_ref, place_ref[1], (held_ref,), cache_ref, sems)


def rest_kernel(place_ref, starts_ref, one_ref, two_ref, _, cache_ref, sems):
    to_cache(place_ref, starts_ref, 1 - place_ref[1], (one_ref, two_ref), cache_ref, sems)


def shape(dims, kind):
    return jax.ShapeDtypeStruct(dims, kind)


def per_device(
    conv_out,
    gate_in,
    residual,
    xproj_weight,
    dtproj_weight,
    dt_bias,
    a_log,
    d_skip,
    init_state,
    out_weight,
    norm_gain,
    kv_weight,
    owner,
    block_start,
    block_count,
):
    tp_count = lax.axis_size("tp")
    ctx_count = lax.axis_size("ctx")
    tokens, chans = conv_out.shape
    feats = residual.shape[1]
    pairs = tp_count // 2
    place = lax.axis_index("ctx")
    member = lax.axis_index("tp")
    core = member % 2
    places = jnp.stack(
        [
            place, core, place * tp_count + member,
            member // (2 * SIDE), (member // 2) % SIDE,
        ]
    ).astype(jnp.int32)
    partner = [(i, i ^ 1) for i in range(tp_count)]

    def line(stage, value_of):
        return [
            lax.ppermute(
                value_of(shift),
                "tp",
                [
                    (
                        (x * SIDE + y) * 2 + c,
                        ((x + shift) % SIDE * SIDE + y) * 2 + c
                        if c == stage
                        else (x * SIDE + (y + shift) % SIDE) * 2 + c,
                    )
                    for x in range(SIDE)
                    for y in range(SIDE)
                    for c in range(2)
                ],
            )
            for shift in range(1, SIDE)
        ]

    def swap(value):
        return lax.ppermute(value, "tp", partner)

    own_gain = norm_gain.reshape(1, feats)
    got_gain, got_weight = swap(own_gain), swap(kv_weight)
    devices = owner.shape[0]
    matches = owner[:, None] == jnp.arange(devices, dtype=jnp.int32)[None, :]
    starts = jnp.sum(jnp.where(matches, block_start[:, None], 0), axis=0)
    counts = jnp.sum(jnp.where(matches, block_count[:, None], 0), axis=0)

    def add(name, kind, *values):
        return pl.pallas_call(
            add_kernel,
            out_shape=shape(values[0].shape, kind),
            compiler_params=params(8),
            name=name,
        )(*values)

    def project(name, give, kind):
        return pl.pallas_call(
            functools.partial(project_kernel, give),
            in_specs=[SM] + [VM] * 2,
            out_shape=shape((BLK + 16, DTR), kind),
            compiler_params=params(8),
            name=name,
        )(places, conv_out, xproj_weight.T)

    give_share = project("project_give", True, BF)
    kept_share = project("project_keep", False, F32)
    got_share, got_gain = lax.optimization_barrier((swap(give_share), got_gain))
    chip = add("chip", BF, kept_share, got_share)
    row = add("row", BF, chip, *line(0, lambda shift: chip))
    own_proj = add("plane", BF, row, *line(1, lambda shift: row))

    blocks = tokens // CHUNK
    step, states, ends = pl.pallas_call(
        first_kernel,
        out_shape=(
            shape((tokens, chans), F32),
            shape((blocks, 2 * STATE, CHUNK), F32),
            shape((STATE + 8, chans), F32),
        ),
        in_specs=[SM] + [VM] * 6,
        scratch_shapes=[
            pltpu.VMEM((tokens, DTR), BF),
            pltpu.VMEM((tokens, chans), F32),
        ],
        compiler_params=params(8),
        name="first",
    )(places, own_proj, swap(own_proj), dtproj_weight, dt_bias.reshape(1, chans), a_log, conv_out)
    def ranges_back(value):
        return [
            lax.ppermute(value, "ctx", [(z, (z + s) % ctx_count) for z in range(ctx_count)])
            for s in range(1, ctx_count)
        ]

    near_weight = pl.pallas_call(
        bring_kernel,
        in_specs=[ANY] * 2,
        out_shape=shape(out_weight.shape, BF),
        scratch_shapes=[pltpu.SemaphoreType.DMA((PIECES,))],
        compiler_params=params(42),
        name="bring",
    )(out_weight, ends)
    partial = (pairs, tokens // 2, 2 * feats)
    half = (pairs // 2,) + partial[1:]
    soon, give, kept = pl.pallas_call(
        give_kernel,
        in_specs=[SM] + [VM] * 12,
        out_shape=(shape(half, BF), shape(half, BF), shape((tokens // 2, chans), BF)),
        scratch_shapes=[
            pltpu.VMEM((tokens, chans), F32),
            pltpu.VMEM((tokens, chans), F32),
            pltpu.VMEM((2, tokens // 2, chans), BF),
        ],
        compiler_params=params(20),
        name="give",
    )(
        places, step, states, a_log, conv_out, gate_in, d_skip.reshape(1, chans), init_state,
        *ranges_back(ends), near_weight, residual,
    )
    got_soon, got = swap(soon), swap(give)
    keep = pl.pallas_call(
        keep_kernel,
        in_specs=[SM, VM, VM],
        out_shape=shape(partial, BF),
        compiler_params=params(16),
        name="keep",
    )(places, kept, near_weight)
    quarter = shape((SIDE, tokens // 2, 2 * feats), BF)
    def pair(name, fars, got):
        return pl.pallas_call(
            functools.partial(pair_kernel, fars),
            out_shape=(quarter,) * 2,
            compiler_params=params(12),
            name=name,
        )(keep, got)

    sums = dict(zip(SOON, pair("pair_soon", SOON, got_soon), strict=True))
    sums.update(zip(LATER, pair("pair", LATER, got), strict=True))
    row = (tokens // 2, 2 * feats)
    parts = pl.pallas_call(
        line_kernel,
        out_shape=(shape(row, F32),) + (shape(row, BF),) * (SIDE - 1),
        compiler_params=params(12),
        name="line",
    )(sums[0], *line(0, lambda shift: sums[shift]))
    parts = [parts[0]] + line(1, lambda shift: parts[shift])

    block_shape = shape((tokens // 2, feats), BF)
    own_layer, other_layer, *kv_terms = pl.pallas_call(
        layer_kernel,
        in_specs=[SM] + [VM] * 9,
        out_shape=(block_shape,) * 2 + (shape((SIDE, BLK + 16, HEAD), BF),) * SIDE,
        scratch_shapes=[pltpu.VMEM((tokens // 2, 2 * KVH * HEAD), BF)],
        compiler_params=params(8),
        name="layer",
    )(places, *parts, residual, own_gain, got_gain, kv_weight, got_weight)
    got_layer = swap(other_layer)
    kv_row = add("kv", BF, kv_terms[0], *line(0, lambda shift: kv_terms[shift]))
    tile, layer_out = pl.pallas_call(
        tile_kernel,
        in_specs=[SM] + [VM] * 6,
        out_shape=(shape((SIDE, BLK, HEAD), BF), shape((tokens, feats), BF)),
        compiler_params=params(8),
        name="tile",
    )(places, kv_row, *line(1, lambda shift: kv_row), own_layer, got_layer)
    stacked = pl.pallas_call(
        stack_kernel,
        in_specs=[SM] + [VM] * 4,
        out_shape=shape((ctx_count, SIDE, BLK, HEAD), BF),
        compiler_params=params(4),
        name="stack",
    )(places, tile, *ranges_back(tile))
    everything = [stacked] + line(0, lambda shift: stacked)
    chosen = (2, 2 * SIDE, BLK, HEAD)
    sems = pltpu.SemaphoreType.DMA((2, SIDE))
    cache_shape = shape((CAP, SIDE, SIDE, BLK, HEAD), BF)

    def for_partner(name, *sources):
        return swap(
            pl.pallas_call(
                pick_kernel,
                in_specs=[SM] * 3 + [VM] * 2,
                out_shape=shape(chosen, BF),
                compiler_params=params(4),
                name=name,
            )(places, starts, counts, *sources)
        )

    got_first = for_partner("pick0", everything[0], everything[EARLY])
    *late, got_first = lax.optimization_barrier((*[everything[i] for i in LATE], got_first))
    everything = [everything[0], everything[EARLY], *late]
    got_last = for_partner("pick1", *late)
    kv_cache = pl.pallas_call(
        own_kernel,
        in_specs=[SM] * 3 + [VM] * SIDE,
        out_specs=ANY,
        out_shape=cache_shape,
        scratch_shapes=[pltpu.VMEM((2, 4 * SIDE, BLK, HEAD), BF), sems],
        compiler_params=params(8),
        name="own",
    )(places, starts, counts, *everything)
    kv_cache = pl.pallas_call(
        rest_kernel,
        in_specs=[SM] * 2 + [VM, VM, ANY],
        out_specs=ANY,
        out_shape=cache_shape,
        input_output_aliases={4: 0},
        scratch_shapes=[sems],
        compiler_params=params(4),
        name="rest",
    )(places, starts, got_first, got_last, kv_cache)
    return (layer_out, kv_cache.reshape(1, CAP, 2 * KVH, BLK, HEAD))


def solution(mesh):
    placed = (
        P("ctx", "tp"),
        P("ctx", "tp"),
        P("ctx", "tp"),
        P("tp", None),
        P(None, "tp"),
        P("tp"),
        P(None, "tp"),
        P("tp"),
        P(None, "tp"),
        P("tp", None),
        P("tp"),
        P("tp", None),
        P(),
        P(),
        P(),
    )
    return jax.shard_map(
        per_device,
        mesh=mesh,
        in_specs=placed,
        out_specs=(P("ctx", "tp"), P(("ctx", "tp"), None, None, None, None)),
        check_vma=False,
    )
```

```python
import functools

import jax
import jax.numpy as jnp
from jax import lax
from jax.experimental import pallas as pl
from jax.experimental.pallas import tpu as pltpu
from jax.sharding import PartitionSpec as P

D = 8192
STATE = 16
DTR = 512
KVH = 8
HEAD = 128
BLK = 128
CAP = 4
EPS = 1e-05
LOG2E = 1.4426950408889634
CHUNK = 64
PIECES = 8
SIDE = 4
SOON, LATER = (2, 3), (0, 1)
EARLY, LATE = 3, (1, 2)
BF = jnp.bfloat16
F32 = jnp.float32

VM = pl.BlockSpec(memory_space=pltpu.VMEM)
SM = pl.BlockSpec(memory_space=pltpu.SMEM)
ANY = pl.BlockSpec(memory_space=pl.ANY)


def params(mib):
    return pltpu.CompilerParams(vmem_limit_bytes=mib * 1024 * 1024)


def project_kernel(give, place_ref, conv_ref, weight_ref, out_ref):
    half = 1 - place_ref[1] if give else place_ref[1]
    conv = conv_ref[pl.ds(pl.multiple_of(half * BLK, BLK), BLK), :]
    both = (((1,), (1,)), ((), ()))
    out_ref[:BLK, :] = lax.dot_general(
        conv, weight_ref[:DTR, :], both, preferred_element_type=F32
    ).astype(out_ref.dtype)
    states = lax.dot_general(weight_ref[DTR:, :], conv, both, preferred_element_type=F32)
    packed = [states[i * 8 : (i + 1) * 8, :] for i in range(DTR // BLK)]
    packed = jnp.concatenate(packed, axis=1)
    out_ref[BLK:, :] = jnp.concatenate([packed, jnp.zeros_like(packed)], axis=0).astype(out_ref.dtype)


def add_kernel(*refs):
    total = refs[0][...].astype(F32)
    for ref in refs[1:-1]:
        total = total + ref[...].astype(F32)
    refs[-1][...] = total.astype(refs[-1].dtype)


def fold_rows(values):
    row = lax.broadcasted_iota(jnp.int32, values[0].shape, 0)
    for reach in (4, 2, 1):
        near = row % (2 * reach) < reach
        values = [
            jnp.where(near, a, b)
            + jnp.where(near, pltpu.roll(a, 8 - reach, 0), pltpu.roll(b, reach, 0))
            for a, b in zip(values[:reach], values[reach:], strict=True)
        ]
    return values[0]


def advance_block(block, hidden, step_ref, drive_ref, states_ref, rates, read_out):
    states = states_ref[block]
    for group in range(CHUNK // 8):
        rows = pl.ds(pl.multiple_of(block * CHUNK + group * 8, 8), 8)
        steps, drives = step_ref[rows, :], drive_ref[rows, :]
        outs = []
        for i in range(8):
            at = group * 8 + i
            decay = jnp.exp2(steps[i : i + 1, :] * rates)
            hidden = decay * hidden + states[:STATE, at : at + 1] * drives[i : i + 1, :]
            if read_out is not None:
                terms = hidden * states[STATE:, at : at + 1]
                outs.append(terms[:8] + terms[8:])
        if read_out is not None:
            read_out[rows, :] = fold_rows(outs)
    return hidden


def first_kernel(
    place_ref, own_proj_ref, got_proj_ref, weight_ref, bias_ref, alog_ref, conv_ref,
    step_ref, states_ref, ends_ref, proj_ref, drive_ref,
):
    tokens = step_ref.shape[0]
    for ref, half in ((own_proj_ref, place_ref[1]), (got_proj_ref, 1 - place_ref[1])):
        proj_ref[pl.ds(pl.multiple_of(half * BLK, BLK), BLK), :] = ref[:BLK, :]
        packed = ref[BLK:, :].astype(F32)
        for group in range(DTR // BLK):
            for block in range(BLK // CHUNK):
                at = group * BLK + block * CHUNK
                states_ref[half * (BLK // CHUNK) + block, group * 8 : (group + 1) * 8, :] = (
                    packed[:8, at : at + CHUNK]
                )
    step = jax.nn.softplus(
        jnp.dot(proj_ref[...], weight_ref[...], preferred_element_type=F32) + bias_ref[...]
    )
    step_ref[...] = step
    drive_ref[...] = step * conv_ref[...].astype(F32)
    rates = -jnp.exp(alog_ref[...]) * LOG2E
    hidden = lax.fori_loop(
        0,
        tokens // CHUNK,
        lambda k, h: advance_block(k, h, step_ref, drive_ref, states_ref, rates, None),
        jnp.zeros_like(rates),
    )
    ends_ref[:STATE, :] = hidden
    ends_ref[STATE:, :] = jnp.broadcast_to(jnp.sum(step, axis=0, keepdims=True), (8, step.shape[1]))


def give_kernel(
    place_ref, step_ref, states_ref, alog_ref, conv_ref, gate_ref, skip_ref, init_ref,
    near_ref, mid_ref, far_ref, weight_ref, residual_ref,
    soon_ref, give_ref, kept_ref, drive_ref, scan_ref, gated_ref,
):
    tokens = step_ref.shape[0]
    place, core = place_ref[0], place_ref[1]
    rates = -jnp.exp(alog_ref[...]) * LOG2E
    hidden = init_ref[...]
    for back, ref in ((3, far_ref), (2, mid_ref), (1, near_ref)):
        passed = jnp.exp2(ref[STATE : STATE + 1, :] * rates) * hidden + ref[:STATE, :]
        hidden = jnp.where(place >= back, passed, hidden)
    drive_ref[...] = step_ref[...] * conv_ref[...].astype(F32)
    lax.fori_loop(
        0,
        tokens // CHUNK,
        lambda k, h: advance_block(k, h, step_ref, drive_ref, states_ref, rates, scan_ref),
        hidden,
    )
    gate = gate_ref[...].astype(F32)
    gated_ref[...] = (
        (scan_ref[...] + skip_ref[...] * conv_ref[...].astype(F32)) * (gate / (1.0 + jnp.exp(-gate)))
    ).astype(BF).reshape(gated_ref.shape)
    kept_ref[...] = gated_ref[core]
    through(place_ref, 1 - core, gated_ref.at[1 - core], weight_ref, ((SOON, soon_ref), (LATER, give_ref)))
    rows, feats = residual_ref.shape[0] // 2, residual_ref.shape[1]
    mine = pl.ds(pl.multiple_of(core * feats, feats), feats)
    other = residual_ref[pl.ds(pl.multiple_of((1 - core) * rows, rows), rows), :]
    give_ref[0, :, mine] = (give_ref[0, :, mine].astype(F32) + other.astype(F32)).astype(BF)


def bring_kernel(weight_ref, _, held_ref, sems):
    wide = weight_ref.shape[1] // PIECES
    copies = [
        pltpu.make_async_copy(
            weight_ref.at[:, pl.ds(i * wide, wide)], held_ref.at[:, pl.ds(i * wide, wide)],
            sems.at[i],
        )
        for i in range(PIECES)
    ]
    for copy in copies:
        copy.start()
    for copy in copies:
        copy.wait()


def through(place_ref, core, gated_ref, weight_ref, parts):
    for fars, out_ref in parts:
        wide = out_ref.shape[2]
        for i, far in enumerate(fars):
            for near in range(SIDE):
                x = lax.rem(place_ref[3] + jnp.where(core == 0, far, near), SIDE)
                y = lax.rem(place_ref[4] + jnp.where(core == 0, near, far), SIDE)
                columns = pl.ds(pl.multiple_of((x * SIDE + y) * wide, wide), wide)
                out_ref[i * SIDE + near] = jnp.dot(
                    gated_ref[...], weight_ref[:, columns], preferred_element_type=F32
                ).astype(BF)


def keep_kernel(place_ref, kept_ref, weight_ref, keep_ref):
    through(place_ref, place_ref[1], kept_ref, weight_ref, ((range(SIDE), keep_ref),))


def pair_kernel(fars, keep_ref, got_ref, *out_refs):
    for i, (far, ref) in enumerate(zip(fars, out_refs, strict=True)):
        kept = keep_ref[far * SIDE : (far + 1) * SIDE]
        got = got_ref[i * SIDE : (i + 1) * SIDE]
        ref[...] = (kept.astype(F32) + got.astype(F32)).astype(ref.dtype)


def line_kernel(own_ref, one_ref, two_ref, three_ref, *out_refs):
    for shift, ref in enumerate(out_refs):
        total = own_ref[shift].astype(F32)
        for other in (one_ref, two_ref, three_ref):
            total = total + other[shift].astype(F32)
        ref[...] = total.astype(ref.dtype)


def layer_kernel(
    place_ref, own_part_ref, one_ref, two_ref, three_ref, residual_ref, own_gain_ref,
    got_gain_ref, own_weight_ref, got_weight_ref, own_ref, other_ref, *rest,
):
    *out_refs, term_ref = rest
    mixed = own_part_ref[...]
    for ref in (one_ref, two_ref, three_ref):
        mixed = mixed + ref[...].astype(F32)
    half = mixed.shape[1] // 2
    first = place_ref[1] == 0
    left, right = mixed[:, :half], mixed[:, half:]
    rows = mixed.shape[0]
    residual = residual_ref[pl.ds(pl.multiple_of(place_ref[1] * rows, rows), rows), :].astype(F32)
    term, squares = 0.0, 0.0
    for piece, gain_ref, weight_ref, layer_ref in (
        (jnp.where(first, left, right) + residual, own_gain_ref, own_weight_ref, own_ref),
        (jnp.where(first, right, left), got_gain_ref, got_weight_ref, other_ref),
    ):
        layer = piece.astype(BF)
        layer_ref[...] = layer
        stream = layer.astype(F32)
        square = stream * stream
        upper = square.astype(BF)
        for value in (upper, (square - upper.astype(F32)).astype(BF)):
            squares = squares + lax.dot_general(
                jnp.ones((16, half), BF), value, (((1,), (1,)), ((), ())),
                preferred_element_type=F32,
            )
        term = term + jnp.dot(
            (stream * gain_ref[...]).astype(BF), weight_ref[...], preferred_element_type=F32
        )
    term_ref[...] = term.astype(BF)
    squares = squares.astype(BF)
    first_axis = jnp.where(first, place_ref[3], place_ref[4])
    for shift, ref in enumerate(out_refs):
        far = lax.rem(first_axis + shift, SIDE)
        for second in range(SIDE):
            j = jnp.where(first, far * SIDE + second, second * SIDE + far)
            ref[second, :BLK, :] = term_ref[:, pl.ds(pl.multiple_of(j * HEAD, HEAD), HEAD)]
            ref[second, BLK:, :] = squares


def tile_kernel(
    place_ref, own_part_ref, one_ref, two_ref, three_ref, own_layer_ref, got_layer_ref,
    tile_ref, layer_ref,
):
    for ref, half in ((own_layer_ref, place_ref[1]), (got_layer_ref, 1 - place_ref[1])):
        rows = ref.shape[0]
        layer_ref[pl.ds(pl.multiple_of(half * rows, rows), rows), :] = ref[...]
    total = own_part_ref[...].astype(F32)
    for ref in (one_ref, two_ref, three_ref):
        total = total + ref[...].astype(F32)
    scale = lax.rsqrt(total[0, BLK : BLK + 1, :] / D + EPS)
    column = jnp.transpose(jnp.broadcast_to(scale, (BLK, BLK)))
    tile_ref[...] = (total[:, :BLK, :] * column[None]).astype(BF)


def choose(place_ref, target, starts_ref, counts_ref, sources, out_ref):
    first, count = starts_ref[target], counts_ref[target]
    slot = lax.rem(place_ref[1] + first, 2)
    for i, ref in enumerate(sources):
        for second in range(SIDE):
            for k in range(2):
                at = slot + 2 * k
                tile = ref[jnp.minimum((first + at) // 2, SIDE - 1), second]
                out_ref[k, i * SIDE + second] = jnp.where(at < count, tile, jnp.zeros_like(tile))


def to_cache(place_ref, starts_ref, core, source_refs, cache_ref, sems):
    slot = lax.rem(core + starts_ref[place_ref[2]], 2)
    waits = []
    for i, shift in enumerate((0, EARLY, *LATE)):
        source_ref = source_refs[i // (SIDE // len(source_refs))]
        first_axis = lax.rem(jnp.where(core == 0, place_ref[3], place_ref[4]) + SIDE - shift, SIDE)
        at = i * SIDE % source_ref.shape[1]
        for k in range(2):
            part = source_ref.at[k, pl.ds(at, SIDE)]
            along_y = pltpu.make_async_copy(
                part, cache_ref.at[slot + 2 * k, first_axis], sems.at[k, i]
            )
            along_x = pltpu.make_async_copy(
                part, cache_ref.at[slot + 2 * k, :, first_axis], sems.at[k, i]
            )
            pl.when(core == 0)(along_y.start)
            pl.when(core == 1)(along_x.start)
            waits.append(along_y)
    for copy in waits:
        copy.wait()


def stack_kernel(place_ref, own_ref, near_ref, mid_ref, far_ref, out_ref):
    for back, ref in enumerate((own_ref, near_ref, mid_ref, far_ref)):
        out_ref[lax.rem(place_ref[0] + SIDE - back, SIDE)] = ref[...]


def pick_kernel(place_ref, starts_ref, counts_ref, one_ref, two_ref, out_ref):
    partner = place_ref[2] + 1 - 2 * place_ref[1]
    choose(place_ref, partner, starts_ref, counts_ref, (one_ref, two_ref), out_ref)


def own_kernel(place_ref, starts_ref, counts_ref, q0, q1, q2, q3, cache_ref, held_ref, sems):
    choose(place_ref, place_ref[2], starts_ref, counts_ref, (q0, q1, q2, q3), held_ref)
    to_cache(place_ref, starts_ref, place_ref[1], (held_ref,), cache_ref, sems)


def rest_kernel(place_ref, starts_ref, one_ref, two_ref, _, cache_ref, sems):
    to_cache(place_ref, starts_ref, 1 - place_ref[1], (one_ref, two_ref), cache_ref, sems)


def shape(dims, kind):
    return jax.ShapeDtypeStruct(dims, kind)


def per_device(
    conv_out,
    gate_in,
    residual,
    xproj_weight,
    dtproj_weight,
    dt_bias,
    a_log,
    d_skip,
    init_state,
    out_weight,
    norm_gain,
    kv_weight,
    owner,
    block_start,
    block_count,
):
    tp_count = lax.axis_size("tp")
    ctx_count = lax.axis_size("ctx")
    tokens, chans = conv_out.shape
    feats = residual.shape[1]
    pairs = tp_count // 2
    place = lax.axis_index("ctx")
    member = lax.axis_index("tp")
    core = member % 2
    places = jnp.stack(
        [
            place, core, place * tp_count + member,
            member // (2 * SIDE), (member // 2) % SIDE,
        ]
    ).astype(jnp.int32)
    partner = [(i, i ^ 1) for i in range(tp_count)]

    def line(stage, value_of):
        return [
            lax.ppermute(
                value_of(shift),
                "tp",
                [
                    (
                        (x * SIDE + y) * 2 + c,
                        ((x + shift) % SIDE * SIDE + y) * 2 + c
                        if c == stage
                        else (x * SIDE + (y + shift) % SIDE) * 2 + c,
                    )
                    for x in range(SIDE)
                    for y in range(SIDE)
                    for c in range(2)
                ],
            )
            for shift in range(1, SIDE)
        ]

    def swap(value):
        return lax.ppermute(value, "tp", partner)

    own_gain = norm_gain.reshape(1, feats)
    got_gain, got_weight = swap(own_gain), swap(kv_weight)
    devices = owner.shape[0]
    matches = owner[:, None] == jnp.arange(devices, dtype=jnp.int32)[None, :]
    starts = jnp.sum(jnp.where(matches, block_start[:, None], 0), axis=0)
    counts = jnp.sum(jnp.where(matches, block_count[:, None], 0), axis=0)

    def add(name, kind, *values):
        return pl.pallas_call(
            add_kernel,
            out_shape=shape(values[0].shape, kind),
            compiler_params=params(8),
            name=name,
        )(*values)

    def project(name, give, kind):
        return pl.pallas_call(
            functools.partial(project_kernel, give),
            in_specs=[SM] + [VM] * 2,
            out_shape=shape((BLK + 16, DTR), kind),
            compiler_params=params(8),
            name=name,
        )(places, conv_out, xproj_weight.T)

    give_share = project("project_give", True, BF)
    kept_share = project("project_keep", False, F32)
    got_share, got_gain = lax.optimization_barrier((swap(give_share), got_gain))
    chip = add("chip", BF, kept_share, got_share)
    row = add("row", BF, chip, *line(0, lambda shift: chip))
    own_proj = add("plane", BF, row, *line(1, lambda shift: row))

    blocks = tokens // CHUNK
    step, states, ends = pl.pallas_call(
        first_kernel,
        out_shape=(
            shape((tokens, chans), F32),
            shape((blocks, 2 * STATE, CHUNK), F32),
            shape((STATE + 8, chans), F32),
        ),
        in_specs=[SM] + [VM] * 6,
        scratch_shapes=[
            pltpu.VMEM((tokens, DTR), BF),
            pltpu.VMEM((tokens, chans), F32),
        ],
        compiler_params=params(8),
        name="first",
    )(places, own_proj, swap(own_proj), dtproj_weight, dt_bias.reshape(1, chans), a_log, conv_out)
    def ranges_back(value):
        return [
            lax.ppermute(value, "ctx", [(z, (z + s) % ctx_count) for z in range(ctx_count)])
            for s in range(1, ctx_count)
        ]

    near_weight = pl.pallas_call(
        bring_kernel,
        in_specs=[ANY] * 2,
        out_shape=shape(out_weight.shape, BF),
        scratch_shapes=[pltpu.SemaphoreType.DMA((PIECES,))],
        compiler_params=params(42),
        name="bring",
    )(out_weight, ends)
    partial = (pairs, tokens // 2, 2 * feats)
    half = (pairs // 2,) + partial[1:]
    soon, give, kept = pl.pallas_call(
        give_kernel,
        in_specs=[SM] + [VM] * 12,
        out_shape=(shape(half, BF), shape(half, BF), shape((tokens // 2, chans), BF)),
        scratch_shapes=[
            pltpu.VMEM((tokens, chans), F32),
            pltpu.VMEM((tokens, chans), F32),
            pltpu.VMEM((2, tokens // 2, chans), BF),
        ],
        compiler_params=params(20),
        name="give",
    )(
        places, step, states, a_log, conv_out, gate_in, d_skip.reshape(1, chans), init_state,
        *ranges_back(ends), near_weight, residual,
    )
    got_soon, got = swap(soon), swap(give)
    keep = pl.pallas_call(
        keep_kernel,
        in_specs=[SM, VM, VM],
        out_shape=shape(partial, BF),
        compiler_params=params(16),
        name="keep",
    )(places, kept, near_weight)
    quarter = shape((SIDE, tokens // 2, 2 * feats), BF)
    def pair(name, fars, got):
        return pl.pallas_call(
            functools.partial(pair_kernel, fars),
            out_shape=(quarter,) * 2,
            compiler_params=params(12),
            name=name,
        )(keep, got)

    sums = dict(zip(SOON, pair("pair_soon", SOON, got_soon), strict=True))
    sums.update(zip(LATER, pair("pair", LATER, got), strict=True))
    row = (tokens // 2, 2 * feats)
    parts = pl.pallas_call(
        line_kernel,
        out_shape=(shape(row, F32),) + (shape(row, BF),) * (SIDE - 1),
        compiler_params=params(12),
        name="line",
    )(sums[0], *line(0, lambda shift: sums[shift]))
    parts = [parts[0]] + line(1, lambda shift: parts[shift])

    block_shape = shape((tokens // 2, feats), BF)
    own_layer, other_layer, *kv_terms = pl.pallas_call(
        layer_kernel,
        in_specs=[SM] + [VM] * 9,
        out_shape=(block_shape,) * 2 + (shape((SIDE, BLK + 16, HEAD), BF),) * SIDE,
        scratch_shapes=[pltpu.VMEM((tokens // 2, 2 * KVH * HEAD), BF)],
        compiler_params=params(8),
        name="layer",
    )(places, *parts, residual, own_gain, got_gain, kv_weight, got_weight)
    got_layer = swap(other_layer)
    kv_row = add("kv", BF, kv_terms[0], *line(0, lambda shift: kv_terms[shift]))
    tile, layer_out = pl.pallas_call(
        tile_kernel,
        in_specs=[SM] + [VM] * 6,
        out_shape=(shape((SIDE, BLK, HEAD), BF), shape((tokens, feats), BF)),
        compiler_params=params(8),
        name="tile",
    )(places, kv_row, *line(1, lambda shift: kv_row), own_layer, got_layer)
    stacked = pl.pallas_call(
        stack_kernel,
        in_specs=[SM] + [VM] * 4,
        out_shape=shape((ctx_count, SIDE, BLK, HEAD), BF),
        compiler_params=params(4),
        name="stack",
    )(places, tile, *ranges_back(tile))
    everything = [stacked] + line(0, lambda shift: stacked)
    chosen = (2, 2 * SIDE, BLK, HEAD)
    sems = pltpu.SemaphoreType.DMA((2, SIDE))
    cache_shape = shape((CAP, SIDE, SIDE, BLK, HEAD), BF)

    def for_partner(name, *sources):
        return swap(
            pl.pallas_call(
                pick_kernel,
                in_specs=[SM] * 3 + [VM] * 2,
                out_shape=shape(chosen, BF),
                compiler_params=params(4),
                name=name,
            )(places, starts, counts, *sources)
        )

    got_first = for_partner("pick0", everything[0], everything[EARLY])
    *late, got_first = lax.optimization_barrier((*[everything[i] for i in LATE], got_first))
    everything = [everything[0], everything[EARLY], *late]
    got_last = for_partner("pick1", *late)
    kv_cache = pl.pallas_call(
        own_kernel,
        in_specs=[SM] * 3 + [VM] * SIDE,
        out_specs=ANY,
        out_shape=cache_shape,
        scratch_shapes=[pltpu.VMEM((2, 4 * SIDE, BLK, HEAD), BF), sems],
        compiler_params=params(8),
        name="own",
    )(places, starts, counts, *everything)
    kv_cache = pl.pallas_call(
        rest_kernel,
        in_specs=[SM] * 2 + [VM, VM, ANY],
        out_specs=ANY,
        out_shape=cache_shape,
        input_output_aliases={4: 0},
        scratch_shapes=[sems],
        compiler_params=params(4),
        name="rest",
    )(places, starts, got_first, got_last, kv_cache)
    return (layer_out, kv_cache.reshape(1, CAP, 2 * KVH, BLK, HEAD))


def solution(mesh):
    placed = (
        P("ctx", "tp"),
        P("ctx", "tp"),
        P("ctx", "tp"),
        P("tp", None),
        P(None, "tp"),
        P("tp"),
        P(None, "tp"),
        P("tp"),
        P(None, "tp"),
        P("tp", None),
        P("tp"),
        P("tp", None),
        P(),
        P(),
        P(),
    )
    return jax.shard_map(
        per_device,
        mesh=mesh,
        in_specs=placed,
        out_specs=(P("ctx", "tp"), P(("ctx", "tp"), None, None, None, None)),
        check_vma=False,
    )
```
